128 devices in a mesh: samp: 8 (over z, core), term: 16 (over y, x).
Axes of the slice: x: 4, y: 4, z: 4, core: 2. Of those that a mesh axis runs over, the one named last changes fastest.
Arguments:
- basis: bfloat16 [8192, 4096], P('samp', 'term'), may hold values from -0.143631065 to 0.143631065
- strain: float32 [8192, 4096], P(('samp', 'term')), may hold values from -17 to 17
- route: int32 [8192], replicated, may hold values from 0 to 8191, as said below
- chosen: int32 [3], replicated, may hold values from 0 to 63, as said below
Outputs:
- residual: float32 [8192, 4096], P('samp', 'term')
- coefficients: float32 [192, 4096], P(None, 'term')
- scores: float32 [3, 64], P(None, 'term')
The draws below stay inside these ranges and needn't reach their ends.
Inputs may be any that keep to these rules, and one draw needn't show every extreme that they name: route is a permutation of the sample indices; of each aligned block of 64 evolutions exactly 8 go to each aligned block of 1024 samples. `chosen`: the 3 selected blocks are distinct.
All inputs are finite; a program needn't handle non-finite values.
Results may differ from the reference program's by a relative error of at most 0.003.
Values may be sent and summed in bfloat16 or wider, within the bound.
A program may use at most 128 MiB of HBM per device.

```python
import jax
import jax.numpy as jnp
from jax import lax

SAMP_DEV = 1024
BLOCK = 64
REGIONS = 4096
STEPS = 3
NSAMP = 8192
TERMS = 4096
NBLK = 64
N_SAMP = 8
N_TERM = 16


def routing(key):
    sim_rows = SAMP_DEV // N_TERM
    capacity = sim_rows // N_SAMP
    devices = N_SAMP * N_TERM
    key_first, key_second = jax.random.split(jax.random.fold_in(key, 11))
    dev_perm = jax.vmap(lambda subkey: jax.random.permutation(subkey, sim_rows))(jax.random.split(key_first, devices))
    block_perm = jax.vmap(lambda subkey: jax.random.permutation(subkey, SAMP_DEV))(jax.random.split(key_second, N_SAMP))
    device_ids = jnp.arange(devices, dtype=jnp.int32)[:, None]
    source_block = device_ids // N_TERM
    term_source = device_ids % N_TERM
    target_block = dev_perm // capacity
    within = dev_perm % capacity
    arrival = term_source * sim_rows + source_block * capacity + within
    slots = block_perm[target_block, arrival]
    return (target_block * SAMP_DEV + slots).reshape(-1).astype(jnp.int32)


def base_fields(key):
    key_normal = jax.random.fold_in(key, 21)
    key_scale = jax.random.fold_in(key, 23)
    normal_raw = jnp.clip(jax.random.normal(key_normal, (NSAMP, TERMS), jnp.float32), -4.0, 4.0)
    column_scale = jnp.exp(jax.random.uniform(key_scale, (TERMS,), jnp.float32, jnp.log(0.3), jnp.log(3.0)))
    return (normal_raw, column_scale)


def draw_basis(key, part):
    normal_raw, column_scale = base_fields(key)
    raw_field = normal_raw
    return (raw_field * column_scale[None, :] * NSAMP ** (-0.5)).astype(jnp.bfloat16)


def draw_strain(key, part):
    normal_raw, column_scale = base_fields(key)
    sample_of = routing(key)
    key = jax.random.fold_in(key, 2)
    key_map, key_region, key_noise = jax.random.split(key, 3)
    term_map = jax.random.randint(key_map, (REGIONS,), 0, TERMS)
    region_scale = jnp.exp(jax.random.uniform(key_region, (REGIONS,), jnp.float32, jnp.log(0.3), jnp.log(3.0)))
    raw_field = normal_raw
    noise_field = jnp.clip(jax.random.normal(key_noise, (NSAMP, REGIONS), jnp.float32), -4.0, 4.0)
    signal = raw_field[sample_of[:, None], term_map[None, :]]
    return (region_scale[None, :] * (0.8 * signal + 0.6 * noise_field)).astype(jnp.float32)


def draw_route(key, part):
    return routing(key)


def draw_chosen(key, part):
    key = jax.random.fold_in(key, 5)
    key_perm, key_slot = jax.random.split(key)
    others = jax.random.permutation(key_perm, NBLK - 1)[:STEPS].astype(jnp.int32)
    slot = jax.random.randint(key_slot, (), 0, STEPS)
    positions = jnp.arange(STEPS, dtype=jnp.int32)
    return jnp.where(positions == slot, NBLK - 1, others).astype(jnp.int32)


def setup_inputs(seed: int = 0) -> dict:
    splits = jax.random.split(jax.random.key(seed), 5)
    return {
        "basis": draw_basis(jax.random.fold_in(splits[4], 71), 0),
        "strain": draw_strain(jax.random.fold_in(splits[4], 71), 0),
        "route": draw_route(jax.random.fold_in(splits[4], 71), 0),
        "chosen": draw_chosen(jax.random.fold_in(splits[4], 71), 0),
    }


highest = lax.Precision.HIGHEST
epsilon = 1e-06

def block_scores(basis, residual):
    rounded = lax.optimization_barrier(residual.astype(jnp.bfloat16)).astype(jnp.float32)
    basis_wide = basis.astype(jnp.float32).reshape(NSAMP, NBLK, BLOCK)

    def block_mean(block_index):
        columns = lax.dynamic_index_in_dim(basis_wide, block_index, 1, keepdims=False)
        correlation = jnp.dot(columns.T, rounded, precision=highest)
        return jnp.mean(correlation * correlation)
    block_means = lax.map(block_mean, jnp.arange(NBLK, dtype=jnp.int32))
    return jnp.sqrt(block_means + epsilon)

def reference(basis, strain, route, chosen):
    samples = jnp.zeros_like(strain).at[route].set(strain)
    residual = samples.astype(jnp.float32)
    basis_kept = None
    score_rows = []
    coef_rows = []
    for pursuit in range(STEPS):
        score_rows.append(block_scores(basis, residual))
        first_col = (chosen[pursuit] * BLOCK).astype(jnp.int32)
        picked = lax.dynamic_slice_in_dim(basis, first_col, BLOCK, 1).astype(jnp.float32)
        if pursuit > 0:
            projection = jnp.dot(basis_kept.T, picked, precision=highest) / NSAMP
            picked = picked - jnp.dot(basis_kept, projection, precision=highest)
        gram_matrix = jnp.dot(picked.T, picked, precision=highest) / NSAMP
        lower_factor = jnp.linalg.cholesky(gram_matrix)
        normed = lax.linalg.triangular_solve(lower_factor, picked, left_side=False, lower=True, transpose_a=True)
        cross_terms = jnp.dot(picked.T, residual, precision=highest) / NSAMP
        coef_now = lax.linalg.triangular_solve(lower_factor, cross_terms, left_side=True, lower=True)
        residual = residual - jnp.dot(normed, coef_now, precision=highest)
        if pursuit == 0:
            basis_kept = normed
        else:
            basis_kept = jnp.concatenate([basis_kept, normed], axis=1)
        coef_rows.append(coef_now)
    return (residual, jnp.concatenate(coef_rows, axis=0), jnp.stack(score_rows, axis=0))
```

```python
import functools

import jax
import jax.numpy as jnp
from jax import lax
from jax.experimental import pallas as pl
from jax.experimental.pallas import tpu as pltpu
from jax.sharding import PartitionSpec as P

BLOCK = 64
STEPS = 3
EPS = 1e-06
MESH = pl.DeviceIdType.MESH
HIGHEST = lax.Precision.HIGHEST
F32 = jnp.float32
BF16 = jnp.bfloat16


def nn(a, b, precision=None):
    return lax.dot_general(
        a, b, (((1,), (0,)), ((), ())), precision=precision, preferred_element_type=F32
    )


def nt(a, b, precision=None):
    return lax.dot_general(
        a, b, (((1,), (1,)), ((), ())), precision=precision, preferred_element_type=F32
    )


def tn(a, b):
    return lax.dot_general(a, b, (((0,), (0,)), ((), ())), preferred_element_type=F32)


def iota(shape, dim):
    return lax.broadcasted_iota(jnp.int32, shape, dim)


def ones_where(mask):
    return jnp.where(mask, 1.0, 0.0).astype(BF16)


def split(v):
    hi = v.astype(BF16)
    return hi, (v - hi.astype(F32)).astype(BF16)


def inverse_factor(a):
    n = a.shape[0]
    rows, cols = iota((n, n), 0), iota((n, n), 1)
    inv = jnp.where(rows == cols, 1.0, 0.0).astype(F32)
    below = iota((n, 1), 0)
    for j in range(n - 1):
        scale = 1.0 / a[j : j + 1, j : j + 1]
        col = jnp.where(below > j, a[:, j : j + 1], 0.0) * scale
        a, inv = a - col * a[j : j + 1, :], inv - col * inv[j : j + 1, :]
    diag = jnp.sum(jnp.where(rows == cols, a, 0.0), axis=1, keepdims=True)
    return inv / jnp.sqrt(diag)


def body(
    dims, chosen, index, place, basis, strain, residual, coefs, scores,
    ptp, prs, psum, pry, ptf, sorted4, r1, pit, btg, rg, lo, rlo, pa,
    g_in, g_r, g_z, g_out, x_in, x_r, x_z, x_out, h_in, h_r, h_s, h_z,
    c_own, c_send, c_r, c_s, c_z, c_fin, cg, sg, ss, rs,
):
    rk, slab, tslab, bl = dims
    nr, q4, sr = 128 * rk, 32 * rk, 8 * rk
    p3, p2 = 3 * bl, 2 * bl
    half, group = 2 * tslab, tslab // 2
    total = 8 * nr
    s, t = lax.axis_index("samp"), lax.axis_index("term")
    z, c = s // 2, lax.rem(s, 2)
    y, x = t // 4, lax.rem(t, 4)
    me = s * 4 + x

    def at_x(d):
        return (s, y * 4 + lax.rem(x + d, 4))

    def at_y(d):
        return (s, lax.rem(y + d, 4) * 4 + x)

    def at_z(d):
        return (lax.rem(z + d, 4) * 2 + c, t)

    partner = (z * 2 + 1 - c, t)

    used = [0]

    def sems(n):
        used[0] += n
        return used[0] - n

    def copy(src, dst, k, dev):
        return pltpu.make_async_remote_copy(
            src_ref=src, dst_ref=dst, send_sem=ss.at[k], recv_sem=rs.at[k],
            device_id=dev, device_id_type=MESH,
        )

    def start(copies):
        for one in copies:
            one.start()
        return copies

    def wait_recv(copies):
        for one in copies:
            one.wait_recv()

    pending = []

    def go(copies):
        pending.extend(copies)
        return start(copies)

    def peer(p):
        other = lax.rem(me + p, 32)
        return other // 4, lax.rem(other, 4)

    barrier = pltpu.get_barrier_semaphore()

    def greet(p, carry):
        ps, px = peer(p)
        pl.semaphore_signal(
            barrier, inc=1, device_id=(ps, y * 4 + px), device_id_type=MESH
        )
        return carry

    lax.fori_loop(1, 32, greet, 0)
    for d in (1, 2, 3):
        pl.semaphore_signal(barrier, inc=1, device_id=at_y(d), device_id_type=MESH)

    rows = iota((p3, tslab), 0)
    which = jnp.where(rows < bl, chosen[0], jnp.where(rows < p2, chosen[1], chosen[2]))
    target = which * bl + lax.rem(rows, bl) - t * tslab
    select = ones_where(iota((p3, tslab), 1) == target)
    for q in range(4):
        ptp[q] = nt(select, basis[q * q4 : (q + 1) * q4, :]).astype(BF16)

    order = ones_where(iota((sr, sr), 0) == place[...])

    def sort_slab(j, carry):
        for k in range(4):
            at = pl.multiple_of((j * 4 + k) * slab, slab)
            v = strain[:, pl.ds(at, slab)]
            hi, rest = split(v)
            mid, low = split(v - hi.astype(F32))
            sorted4[j, k] = nn(order, hi) + nn(order, mid) + nn(order, low)
        return carry

    lax.fori_loop(0, 4, sort_slab, 0)

    pl.semaphore_wait(barrier, 34)

    k = sems(3)
    p_x = go([copy(ptp.at[lax.rem(x + d, 4)], prs.at[d - 1], k + d - 1, at_x(d)) for d in (1, 2, 3)])

    ka = sems(1)

    def scatter(p, carry):
        ps, px = peer(p)
        copy(
            sorted4.at[:, px, pl.ds(pl.multiple_of(ps * rk, rk), rk), :],
            r1.at[:, pl.ds(pl.multiple_of(me * rk, rk), rk), :],
            ka,
            (ps, y * 4 + px),
        ).start()
        return carry

    lax.fori_loop(1, 32, scatter, 0)
    for j in range(4):
        r1[j, pl.ds(pl.multiple_of(me * rk, rk), rk), :] = sorted4[
            j, x, pl.ds(pl.multiple_of(s * rk, rk), rk), :
        ]

    def build(q, carry):
        at = pl.multiple_of(q * q4, q4)
        pit[pl.ds(at, q4), :] = ones_where(iota((q4, nr), 0) + at == index[...])
        return carry

    lax.fori_loop(0, 4, build, 0)
    eye = ones_where(iota((tslab, tslab), 0) == iota((tslab, tslab), 1))
    bt = nt(eye, basis[...]).astype(BF16)
    mine = pl.ds(pl.multiple_of(x * tslab, tslab), tslab)
    btg[mine, :] = nn(bt, pit[...]).astype(BF16)

    def ring(ref, view, at, dev, k):
        here, left, right = view(ref, at, None), view(ref, lax.rem(at + 3, 4), 0), view(ref, lax.rem(at + 1, 4), 1)
        first = [copy(here, here, k, dev(1)), copy(here, here, k + 1, dev(3))]
        second = [copy(left, left, k + 2, dev(1)), copy(right, right, k + 3, dev(3))]
        return first, second

    def view_b(ref, slot, part):
        if part is None:
            return ref.at[pl.ds(pl.multiple_of(slot * tslab, tslab), tslab), :]
        return ref.at[pl.ds(pl.multiple_of(slot * tslab + part * group, group), group), :]

    def view_r(ref, slot, part):
        rows = pl.ds(pl.multiple_of(slot * q4, q4), q4)
        if part is None:
            return ref.at[:, rows, :]
        return ref.at[2 * part : 2 * part + 2, rows, :]

    b_first, b_second = ring(btg, view_b, x, at_x, sems(4))
    go(b_first)

    wait_recv(p_x)
    psum[...] = ptp[x] + prs[0] + (prs[1] + prs[2])
    k = sems(3)
    p_y = go([copy(psum, pry.at[d - 1], k + d - 1, at_y(d)) for d in (1, 2, 3)])
    wait_recv(p_y)
    ptf[x] = psum[...] + pry[0] + (pry[1] + pry[2])
    k = sems(3)
    p_g = go([copy(ptf.at[x], ptf.at[x], k + d - 1, at_x(d)) for d in (1, 2, 3)])

    pltpu.make_async_copy(
        r1.at[:, pl.ds(0, 31 * rk), :], r1.at[:, pl.ds(0, 31 * rk), :], rs.at[ka]
    ).wait()
    own_rows = pl.ds(pl.multiple_of(y * q4, q4), q4)

    def halves(j, carry):
        hi, low = split(r1[j])
        rg[j, own_rows, :] = hi
        lo[j] = low
        return carry

    lax.fori_loop(0, 4, halves, 0)
    r_first, r_second = ring(rg, view_r, y, at_y, sems(4))
    go(r_first)
    k = sems(3)
    lows = go([copy(lo.at[lax.rem(y + d, 4)], rlo.at[own_rows, :], k + d - 1, at_y(d)) for d in (1, 2, 3)])
    rlo[own_rows, :] = lo[y]

    b_first[0].wait_recv()
    go(b_second[:1])
    b_first[1].wait_recv()
    go(b_second[1:])

    def reduce_pair(src, got, k):
        return go([copy(src.at[1 - c], got, k, partner)])

    def reduce_ring(src, got, parts, k, pair):
        wait_recv(pair)
        parts[z] = src[c] + got[...]
        return go([copy(parts.at[z], parts.at[z], k + d - 1, at_z(d)) for d in (1, 2, 3)])

    def reduce_back(parts, out, k, around):
        wait_recv(around)
        out[c] = (parts[0] + parts[1]) + (parts[2] + parts[3])
        return go([copy(out.at[c], out.at[c], k, partner)])

    wait_recv(p_g)
    at = 0
    for i in range(3):
        for j in range(i + 1):
            acc = None
            for q in range(4):
                one = nt(ptf[q, i * bl : (i + 1) * bl, :], ptf[q, j * bl : (j + 1) * bl, :])
                acc = one if acc is None else acc + one
            g_in[at // 3, at % 3] = acc
            at += 1
    g_1 = reduce_pair(g_in, g_r, sems(1))
    acc = None
    for q in range(4):
        one = nn(ptf[q], pit[q * q4 : (q + 1) * q4, :])
        acc = one if acc is None else acc + one
    pa[...] = acc.astype(BF16)
    g_2 = reduce_ring(g_in, g_r, g_z, sems(3), g_1)

    r_first[0].wait_recv()
    go(r_second[:1])
    r_first[1].wait_recv()
    go(r_second[1:])

    g_3 = reduce_back(g_z, g_out, sems(1), g_2)
    wait_recv(b_second)

    hk = sems(1)
    other_half = pl.ds(pl.multiple_of((1 - c) * half, half), half)
    own_half = pl.ds(pl.multiple_of(c * half, half), half)
    h_in[1] = nt(btg[other_half, :], pa[:p2, :])
    h_1 = go([copy(h_in.at[1], h_r, hk, partner)])
    h_in[0] = nt(btg[own_half, :], pa[:p2, :])

    wait_recv(g_3)
    gram = [g_out[i // 3, i % 3] / total for i in range(6)]
    w00 = inverse_factor(gram[0])
    l10, l20 = nt(gram[1], w00, HIGHEST), nt(gram[3], w00, HIGHEST)
    w11 = inverse_factor(gram[2] - nt(l10, l10, HIGHEST))
    l21 = nt(gram[4] - nt(l20, l10, HIGHEST), w11, HIGHEST)
    w22 = inverse_factor(gram[5] - nt(l20, l20, HIGHEST) - nt(l21, l21, HIGHEST))
    w10 = -nn(w11, nn(l10, w00, HIGHEST), HIGHEST)
    w20 = -nn(w22, nn(l20, w00, HIGHEST) + nn(l21, w10, HIGHEST), HIGHEST)
    w21 = -nn(w22, nn(l21, w11, HIGHEST), HIGHEST)
    zero = jnp.zeros((bl, bl), F32)
    w = jnp.concatenate(
        [
            jnp.concatenate([w00, zero, zero], axis=1),
            jnp.concatenate([w10, w11, zero], axis=1),
            jnp.concatenate([w20, w21, w22], axis=1),
        ],
        axis=0,
    )
    eye3 = jnp.where(iota((p3, p3), 0) == iota((p3, p3), 1), 1.0, 0.0).astype(F32)
    wt = nt(eye3, w, HIGHEST)

    wait_recv(h_1)
    h_s[...] = h_in[0] + h_r[...]

    def part(ref, zz, *lead):
        return ref.at[(*lead, pl.ds(pl.multiple_of(zz * group, group), group), slice(None))]

    k = sems(3)
    h_2 = go([copy(part(h_s, lax.rem(z + d, 4)), h_z.at[d - 1], k + d - 1, at_z(d)) for d in (1, 2, 3)])

    wait_recv(r_second)
    wait_recv(lows)
    x_mine = nn(pa[...], rg[y]) + nn(pa[...], rlo[...])
    x_in[0] = x_mine[: p3 // 2]
    x_in[1] = x_mine[p3 // 2 :]
    x_1 = reduce_pair(x_in, x_r, sems(1))

    ck, cz = sems(4), sems(12)
    c_1, c_2 = [], []

    def correlate(j):
        c_send[j] = nn(btg[other_half, :], rg[j]).astype(BF16)
        c_1.append(go([copy(c_send.at[j], c_r.at[j], ck + j, partner)]))
        c_own[j] = nn(btg[own_half, :], rg[j])

    def pass_on(j):
        wait_recv(c_1[j])
        both = c_own[j] + c_r[j].astype(F32)
        c_own[j] = both
        c_s[j] = both.astype(BF16)
        c_2.append(
            go([copy(part(c_s, lax.rem(z + d, 4), j), c_z.at[j, d - 1], cz + 3 * j + d - 1, at_z(d)) for d in (1, 2, 3)])
        )

    correlate(0)
    x_2 = reduce_ring(x_in, x_r, x_z, sems(3), x_1)
    correlate(1)
    pass_on(0)
    correlate(2)
    pass_on(1)
    x_3 = reduce_back(x_z, x_out, sems(1), x_2)
    correlate(3)
    pass_on(2)
    wait_recv(x_3)
    cross = jnp.concatenate([x_out[0], x_out[1]], axis=0) / total
    coef = nn(w, cross, HIGHEST)
    coefs[...] = coef
    cg[y] = coef[:p2].astype(BF16)
    k = sems(3)
    cg_1 = go([copy(cg.at[y], cg.at[y], k + d - 1, at_y(d)) for d in (1, 2, 3)])
    pass_on(3)

    y_hi, y_lo = split(nn(wt, coef, HIGHEST))
    for q in range(4):
        at = slice(q * q4, (q + 1) * q4)
        fitted = tn(ptf[q], y_hi) + tn(ptf[q], y_lo)
        residual[at, :] = nn(pit[at, :], rg[y]) + nn(pit[at, :], rlo[...]) - fitted

    wait_recv(h_2)
    h_all = part(h_s, z)[...] + h_z[0] + (h_z[1] + h_z[2])
    hn = nt(h_all, w[:p2, :p2], HIGHEST).astype(BF16)
    first = jnp.where(iota((group, p2), 1) < bl, hn.astype(F32), 0.0).astype(BF16)
    wait_recv(cg_1)
    sums = [None] * 3
    for j in range(4):
        wait_recv(c_2[j])
        c0 = part(c_own, z, j)[...] + c_z[j, 0].astype(F32) + (c_z[j, 1].astype(F32) + c_z[j, 2].astype(F32))
        for i, v in enumerate((c0, c0 - nn(first, cg[j]), c0 - nn(hn, cg[j]))):
            sums[i] = v * v if sums[i] is None else sums[i] + v * v
    own_group = c * 4 + z
    per = group // bl
    rows8, lanes8 = iota((8, 128), 0), iota((8, 128), 1)
    tile = jnp.zeros((8, 128), F32)
    for i in range(3):
        for b in range(per):
            value = jnp.sum(sums[i][b * bl : (b + 1) * bl, :], axis=(0, 1), keepdims=True)
            spot = (rows8 == i) & (lanes8 == lax.rem(own_group, 2) * per + b)
            tile = jnp.where(spot, value, tile)
    sg[me] = tile
    ks = sems(1)

    def tell(p, carry):
        ps, px = peer(p)
        copy(sg.at[me], sg.at[me], ks, (ps, y * 4 + px)).start()
        return carry

    lax.fori_loop(1, 32, tell, 0)
    pltpu.make_async_copy(sg.at[pl.ds(0, 31)], sg.at[pl.ds(0, 31)], rs.at[ks]).wait()
    out = jnp.zeros((8, 128), F32)
    for i in range(2):
        grp = 2 * x + i
        src = (lax.rem(grp, 4) * 2 + grp // 4) * 4
        for px in range(4):
            out = out + sg[src + px]
    out = jnp.sqrt(out / (bl * 16 * slab) + EPS)
    scores[...] = out[:3, : 2 * per]

    pltpu.make_async_copy(
        r1.at[:, pl.ds(0, 31 * rk), :], r1.at[:, pl.ds(0, 31 * rk), :], ss.at[ka]
    ).wait()
    pltpu.make_async_copy(sg.at[pl.ds(0, 31)], sg.at[pl.ds(0, 31)], ss.at[ks]).wait()
    for one in pending:
        one.wait_send()


def local(dims, basis, strain, route, chosen):
    rk, slab, tslab, bl = dims
    nr, q4, sr = 128 * rk, 32 * rk, 8 * rk
    p3, p2 = 3 * bl, 2 * bl
    half, group = 2 * tslab, tslab // 2
    s, t = lax.axis_index("samp"), lax.axis_index("term")

    routes = route.reshape(128, sr)
    goes = routes // nr
    hit = goes == s
    before = jnp.tril(jnp.ones((sr, sr), jnp.bool_), -1)
    rank = jnp.sum(jnp.where(before[None], hit[:, None, :], False), axis=2)
    slot = hit[:, :, None] & (rank[:, :, None] == jnp.arange(rk)[None, None, :])
    sample = jnp.sum(jnp.where(slot, (routes - goes * nr)[:, :, None], 0), axis=1)
    index = sample.reshape(8, 4, 4, rk).transpose(1, 0, 2, 3).reshape(1, nr)
    own = lax.dynamic_index_in_dim(goes, s * 16 + t, 0, keepdims=False)
    same = (own[:, None] == own[None, :]) & before
    place = (own * rk + jnp.sum(same, axis=1)).reshape(1, sr)

    vmem = pl.BlockSpec(memory_space=pltpu.VMEM)
    scratch = [
        ((4, p3, q4), BF16), ((3, p3, q4), BF16), ((p3, q4), BF16), ((3, p3, q4), BF16), ((4, p3, q4), BF16),
        ((4, 4, sr, slab), F32), ((4, q4, slab), F32), ((nr, nr), BF16), ((4 * tslab, nr), BF16),
        ((4, nr, slab), BF16), ((4, q4, slab), BF16), ((nr, slab), BF16), ((p3, nr), BF16),
        ((2, 3, bl, bl), F32), ((3, bl, bl), F32), ((4, 3, bl, bl), F32), ((2, 3, bl, bl), F32),
        ((2, p3 // 2, slab), F32), ((p3 // 2, slab), F32), ((4, p3 // 2, slab), F32), ((2, p3 // 2, slab), F32),
        ((2, half, p2), F32), ((half, p2), F32), ((half, p2), F32), ((3, group, p2), F32),
        ((4, half, slab), F32), ((4, half, slab), BF16), ((4, half, slab), BF16), ((4, half, slab), BF16),
        ((4, 3, group, slab), BF16), ((8, 128), F32), ((4, p2, slab), BF16), ((32, 8, 128), F32),
    ]
    return pl.pallas_call(
        functools.partial(body, dims),
        out_shape=(
            jax.ShapeDtypeStruct((nr, slab), F32),
            jax.ShapeDtypeStruct((p3, slab), F32),
            jax.ShapeDtypeStruct((3, tslab // bl), F32),
        ),
        in_specs=[pl.BlockSpec(memory_space=pltpu.SMEM), vmem, vmem, vmem, vmem],
        out_specs=(vmem, vmem, vmem),
        scratch_shapes=[pltpu.VMEM(shape, dtype) for shape, dtype in scratch]
        + [pltpu.SemaphoreType.DMA((64,)), pltpu.SemaphoreType.DMA((64,))],
        compiler_params=pltpu.CompilerParams(
            collective_id=0, has_side_effects=True, vmem_limit_bytes=60 * 1024 * 1024
        ),
    )(chosen, index, place, basis, strain)


def solution(mesh, dims=(8, 256, 256, BLOCK)):
    return jax.shard_map(
        functools.partial(local, dims),
        mesh=mesh,
        in_specs=(P("samp", "term"), P(("samp", "term"), None), P(), P()),
        out_specs=(P("samp", "term"), P(None, "term"), P(None, "term")),
        check_vma=False,
    )
```

```python
import functools

import jax
import jax.numpy as jnp
from jax import lax
from jax.experimental import pallas as pl
from jax.experimental.pallas import tpu as pltpu
from jax.sharding import PartitionSpec as P

BLOCK = 64
STEPS = 3
EPS = 1e-06
MESH = pl.DeviceIdType.MESH
HIGHEST = lax.Precision.HIGHEST
F32 = jnp.float32
BF16 = jnp.bfloat16


def nn(a, b, precision=None):
    return lax.dot_general(
        a, b, (((1,), (0,)), ((), ())), precision=precision, preferred_element_type=F32
    )


def nt(a, b, precision=None):
    return lax.dot_general(
        a, b, (((1,), (1,)), ((), ())), precision=precision, preferred_element_type=F32
    )


def tn(a, b):
    return lax.dot_general(a, b, (((0,), (0,)), ((), ())), preferred_element_type=F32)


def iota(shape, dim):
    return lax.broadcasted_iota(jnp.int32, shape, dim)


def ones_where(mask):
    return jnp.where(mask, 1.0, 0.0).astype(BF16)


def split(v):
    hi = v.astype(BF16)
    return hi, (v - hi.astype(F32)).astype(BF16)


class Bulk:
    def __init__(self, view, send_sem, recv_sem):
        self.view, self.send_sem, self.recv_sem = view, send_sem, recv_sem

    def wait_send(self):
        pltpu.make_async_copy(self.view, self.view, self.send_sem).wait()

    def wait_recv(self):
        pltpu.make_async_copy(self.view, self.view, self.recv_sem).wait()


def inverse_factor(a, width=8):
    n = a.shape[0]
    width = min(width, n)
    rows, cols = iota((n, n), 0), iota((n, n), 1)
    inv = jnp.where(rows == cols, 1.0, 0.0).astype(F32)
    for g in range(0, n, width):
        picked = range(g, g + width)
        columns = [jnp.broadcast_to(a[:, j : j + 1], (n, n)) for j in picked]
        rows_a = [a[j : j + 1, :] for j in picked]
        rows_i = [inv[j : j + 1, :] for j in picked]
        drop_a = drop_i = 0.0
        for i, j in enumerate(picked):
            scale = 1.0 / columns[i][j : j + 1, :]
            unit_a, unit_i = rows_a[i] * scale, rows_i[i] * scale
            below = jnp.where(rows > j, columns[i], 0.0)
            for m in range(i + 1, width):
                factor = columns[i][g + m : g + m + 1, :]
                rows_a[m] = rows_a[m] - factor * unit_a
                rows_i[m] = rows_i[m] - factor * unit_i
                columns[m] = columns[m] - below * (columns[m][j : j + 1, :] * scale)
            drop_a, drop_i = drop_a + below * unit_a, drop_i + below * unit_i
        a, inv = a - drop_a, inv - drop_i
    diag = jnp.sum(jnp.where(rows == cols, a, 0.0), axis=1, keepdims=True)
    return inv / jnp.sqrt(diag)


def body(
    dims, chosen, index, place, basis, strain, residual, coefs, scores,
    ptp, prs, psum, pry, ptf, out_h, mid_h, in_h, out_l, mid_l, in_l, pit, btg, rg, lo, rlo, pa,
    g_in, g_r, g_z, g_out, x_in, x_r, x_z, x_out, v_in, v_r, v_z, v_out, h_in, h_r, h_s, h_z,
    c_own, c_send, c_r, c_s, c_z, cg, sx, sg, wi, wm, wtm, ss, rs,
):
    rk, slab, tslab, bl = dims
    nr, q4, sr = 128 * rk, 32 * rk, 8 * rk
    p3, p2 = 3 * bl, 2 * bl
    half, group, wide = 2 * tslab, tslab // 2, slab // 2
    total = 8 * nr
    s, t = lax.axis_index("samp"), lax.axis_index("term")
    z, c = s // 2, lax.rem(s, 2)
    y, x = t // 4, lax.rem(t, 4)

    def at_x(d):
        return (s, y * 4 + lax.rem(x + d, 4))

    def at_y(d):
        return (s, lax.rem(y + d, 4) * 4 + x)

    def at_s(d):
        return (lax.rem(s + d, 8), t)

    def at_z(d):
        return (lax.rem(z + d, 4) * 2 + c, t)

    partner = (z * 2 + 1 - c, t)

    used = [0]

    def sems(n):
        used[0] += n
        return used[0] - n

    def copy(src, dst, k, dev):
        return pltpu.make_async_remote_copy(
            src_ref=src, dst_ref=dst, send_sem=ss.at[k], recv_sem=rs.at[k],
            device_id=dev, device_id_type=MESH,
        )

    def start(copies):
        for one in copies:
            one.start()
        return copies

    pending, awaited = [], []

    def wait_recv(copies):
        for one in copies:
            one.wait_recv()
            awaited[:] = [other for other in awaited if other is not one]

    def track(copies):
        pending.extend(copies)
        awaited.extend(copies)
        return copies

    def go(copies):
        return start(track(copies))

    def finish():
        wait_recv(list(awaited))
        for one in pending:
            one.wait_send()

    barrier = pltpu.get_barrier_semaphore()

    def greet(dev):
        pl.semaphore_signal(barrier, inc=1, device_id=dev, device_id_type=MESH)

    for d in (1, 2, 3):
        greet(at_x(d))
        greet(at_y(d))
    for d in range(1, 8):
        greet(at_s(d))

    rows = iota((p3, tslab), 0)
    which = jnp.where(rows < bl, chosen[0], jnp.where(rows < p2, chosen[1], chosen[2]))
    target = which * bl + lax.rem(rows, bl) - t * tslab
    select = ones_where(iota((p3, tslab), 1) == target)
    for q in range(4):
        ptp[q] = nt(select, basis[q * q4 : (q + 1) * q4, :]).astype(BF16)

    order = ones_where(iota((sr, sr), 0) == place[...])

    def packed(v):
        pair = [v[:, n * wide : (n + 1) * wide].reshape(8, rk, wide) for n in (0, 1)]
        return jnp.stack(pair, axis=1).reshape(8, 2 * rk, wide).astype(BF16)

    def unpacked(v):
        v = v.astype(F32).reshape(32, 2, rk, wide)
        return jnp.concatenate([v[:, n].reshape(q4, wide) for n in (0, 1)], axis=1).astype(BF16)

    def sort_slab(j, carry):
        for k in range(4):
            at = pl.multiple_of((j * 4 + k) * slab, slab)
            hi, low = split(strain[:, pl.ds(at, slab)])
            out_h[j, :, k] = packed(nn(order, hi))
            out_l[j, :, k] = packed(nn(order, low))
        return carry

    lax.fori_loop(0, 4, sort_slab, 0)

    pl.semaphore_wait(barrier, 13)

    k = sems(3)
    p_1 = go([copy(ptp.at[lax.rem(y + d, 4)], prs.at[d - 1], k + d - 1, at_y(d)) for d in (1, 2, 3)])

    to_s, to_x = {}, {}

    def send_z(low, j):
        src, dst = ((out_h, mid_h), (out_l, mid_l))[low]
        k = sems(1)

        def scatter(d, carry):
            dev = at_s(d)
            copy(src.at[j, dev[0]], dst.at[j, s], k, dev).start()
            return carry

        lax.fori_loop(1, 8, scatter, 0)
        to_s[low, j] = track([Bulk(dst.at[j, pl.ds(0, 7)], ss.at[k], rs.at[k])])
        dst[j, s] = src[j, s]

    def send_x(low, j):
        src, dst = ((mid_h, in_h), (mid_l, in_l))[low]
        wait_recv(to_s[low, j])
        k = sems(3)
        to_x[low, j] = go([copy(src.at[j, :, lax.rem(x + d, 4)], dst.at[j, x], k + d - 1, at_x(d)) for d in (1, 2, 3)])
        dst[j, x] = src[j, :, x]

    send_z(0, 0)
    send_z(0, 1)

    def build(q, carry):
        at = pl.multiple_of(q * q4, q4)
        pit[pl.ds(at, q4), :] = ones_where(iota((q4, nr), 0) + at == index[...])
        return carry

    lax.fori_loop(0, 4, build, 0)
    eye = ones_where(iota((tslab, tslab), 0) == iota((tslab, tslab), 1))
    bt = nt(eye, basis[...]).astype(BF16)
    btg[pl.ds(pl.multiple_of(x * tslab, tslab), tslab), :] = nn(bt, pit[...]).astype(BF16)

    own_rows = pl.ds(pl.multiple_of(y * q4, q4), q4)
    piece = tslab // 4
    b_out, b_on, r_out, r_on = [], [], [], []

    def b_view(slot, i):
        return btg.at[pl.ds(pl.multiple_of(slot * tslab + i * piece, piece), piece), :]

    def r_view(slot, j):
        return rg.at[j, pl.ds(pl.multiple_of(slot * q4, q4), q4), :]

    def ring_out(view, i, at, dev):
        k = sems(2)
        return go([copy(view(at, i), view(at, i), k + n, dev(1 + 2 * n)) for n in (0, 1)])

    def ring_on(view, i, at, dev, out):
        wait_recv([out[i // 2]])
        slot = lax.rem(at + (3, 1)[i // 2], 4)
        k = sems(1)
        return go([copy(view(slot, i), view(slot, i), k, dev((1, 3)[i // 2]))])

    def send_b(i):
        b_out.append(ring_out(b_view, i, x, at_x))

    def pass_b(i):
        b_on.append(ring_on(b_view, i, x, at_x, b_out[i]))

    def send_r(j):
        wait_recv(to_x[0, j])
        rg[j, own_rows, :] = unpacked(in_h[j])
        r_out.append(ring_out(r_view, j, y, at_y))

    def pass_r(j):
        r_on.append(ring_on(r_view, j, y, at_y, r_out[j]))

    send_b(0)
    send_x(0, 0)
    send_z(0, 2)
    wait_recv(p_1)
    psum[...] = ptp[y] + prs[0] + (prs[1] + prs[2])
    k = sems(3)
    p_2 = go([copy(psum, pry.at[d - 1], k + d - 1, at_x(d)) for d in (1, 2, 3)])
    send_b(1)
    send_x(0, 1)
    send_z(0, 3)
    send_r(0)
    pass_b(0)
    wait_recv(p_2)
    ptf[y] = psum[...] + pry[0] + (pry[1] + pry[2])
    k = sems(3)
    p_3 = go([copy(ptf.at[y], ptf.at[y], k + d - 1, at_y(d)) for d in (1, 2, 3)])
    send_x(0, 2)
    send_z(1, 0)
    send_b(2)
    send_r(1)
    pass_r(0)
    pass_b(1)
    send_x(0, 3)
    send_z(1, 1)
    send_b(3)

    def reduce_pair(src, got, k):
        return go([copy(src.at[1 - c], got, k, partner)])

    def reduce_ring(src, got, parts, k, pair):
        wait_recv(pair)
        parts[z] = src[c] + got[...]
        return go([copy(parts.at[z], parts.at[z], k + d - 1, at_z(d)) for d in (1, 2, 3)])

    def reduce_back(parts, out, k, around):
        wait_recv(around)
        out[c] = (parts[0] + parts[1]) + (parts[2] + parts[3])
        return go([copy(out.at[c], out.at[c], k, partner)])

    wait_recv(p_3)
    at = 0
    for i in range(3):
        for j in range(i + 1):
            acc = None
            for q in range(4):
                one = nt(ptf[q, i * bl : (i + 1) * bl, :], ptf[q, j * bl : (j + 1) * bl, :])
                acc = one if acc is None else acc + one
            g_in[at // 3, at % 3] = acc
            at += 1
    g_1 = reduce_pair(g_in, g_r, sems(1))
    send_r(2)
    pass_r(1)
    pass_b(2)
    g_2 = reduce_ring(g_in, g_r, g_z, sems(3), g_1)
    send_z(1, 2)
    send_z(1, 3)
    acc = None
    for q in range(4):
        one = nn(ptf[q], pit[q * q4 : (q + 1) * q4, :])
        acc = one if acc is None else acc + one
    pa[...] = acc.astype(BF16)
    send_r(3)
    pass_r(2)
    pass_b(3)
    g_3 = reduce_back(g_z, g_out, sems(1), g_2)
    for j in range(4):
        send_x(1, j)
    pass_r(3)

    def lows_on():
        for j in range(4):
            wait_recv(to_x[1, j])
            lo[j] = unpacked(in_l[j])
        k = sems(3)
        rlo[own_rows, :] = lo[y]
        return go([copy(lo.at[lax.rem(y + d, 4)], rlo.at[own_rows, :], k + d - 1, at_y(d)) for d in (1, 2, 3)])

    wait_recv(g_3)

    def factor(i, a):
        wi[i] = inverse_factor(a)

    def rest(i, j):
        return g_out[(i * (i + 1) // 2 + j) // 3, (i * (i + 1) // 2 + j) % 3] / total

    factor(0, rest(0, 0))

    def left_over(copies):
        return [got for got in copies if any(got is other for other in awaited)]

    for i in range(4):
        wait_recv(left_over(b_out[i] + b_on[i]))
    hk = sems(1)
    other_half = pl.ds(pl.multiple_of((1 - c) * half, half), half)
    own_half = pl.ds(pl.multiple_of(c * half, half), half)
    h_in[1] = nt(btg[other_half, :], pa[:p2, :])
    h_1 = go([copy(h_in.at[1], h_r, hk, partner)])
    h_in[0] = nt(btg[own_half, :], pa[:p2, :])

    def part(ref, zz, *lead):
        return ref.at[(*lead, pl.ds(pl.multiple_of(zz * group, group), group), slice(None))]

    ck, cz = sems(4), sems(12)
    c_1, c_2 = [], []

    def correlate(j):
        wait_recv(left_over(r_out[j] + r_on[j]))
        c_send[j] = nn(btg[other_half, :], rg[j]).astype(BF16)
        c_1.append(go([copy(c_send.at[j], c_r.at[j], ck + j, partner)]))
        c_own[j] = nn(btg[own_half, :], rg[j])

    def pass_on(j):
        wait_recv(c_1[j])
        both = c_own[j] + c_r[j].astype(F32)
        c_own[j] = both
        c_s[j] = both.astype(BF16)
        c_2.append(
            go([copy(part(c_s, lax.rem(z + d, 4), j), c_z.at[j, d - 1], cz + 3 * j + d - 1, at_z(d)) for d in (1, 2, 3)])
        )

    correlate(0)
    wait_recv(h_1)
    h_s[...] = h_in[0] + h_r[...]
    k = sems(3)
    h_2 = go([copy(part(h_s, lax.rem(z + d, 4)), h_z.at[d - 1], k + d - 1, at_z(d)) for d in (1, 2, 3)])
    pass_on(0)
    w00 = wi[0]
    l10, l20 = nt(rest(1, 0), w00, HIGHEST), nt(rest(2, 0), w00, HIGHEST)
    factor(1, rest(1, 1) - nt(l10, l10, HIGHEST))
    correlate(1)
    lows = lows_on()
    pass_on(1)
    correlate(2)
    w11 = wi[1]
    l21 = nt(rest(2, 1) - nt(l20, l10, HIGHEST), w11, HIGHEST)
    factor(2, rest(2, 2) - nt(l20, l20, HIGHEST) - nt(l21, l21, HIGHEST))
    pass_on(2)
    for j in range(4):
        wait_recv(left_over(r_out[j] + r_on[j]))

    def cross_pair(v, src, got):
        src[0] = v[: p3 // 2]
        src[1] = v[p3 // 2 :]
        return reduce_pair(src, got, sems(1))

    x_1 = cross_pair(nn(pa[...], rg[y]), x_in, x_r)
    correlate(3)
    x_2 = reduce_ring(x_in, x_r, x_z, sems(3), x_1)
    pass_on(3)
    w22 = wi[2]
    w10 = -nn(w11, nn(l10, w00, HIGHEST), HIGHEST)
    w20 = -nn(w22, nn(l20, w00, HIGHEST) + nn(l21, w10, HIGHEST), HIGHEST)
    w21 = -nn(w22, nn(l21, w11, HIGHEST), HIGHEST)
    zero = jnp.zeros((bl, bl), F32)
    wm[...] = jnp.concatenate(
        [
            jnp.concatenate([w00, zero, zero], axis=1),
            jnp.concatenate([w10, w11, zero], axis=1),
            jnp.concatenate([w20, w21, w22], axis=1),
        ],
        axis=0,
    )
    x_3 = reduce_back(x_z, x_out, sems(1), x_2)
    eye3 = jnp.where(iota((p3, p3), 0) == iota((p3, p3), 1), 1.0, 0.0).astype(F32)
    wtm[...] = nt(eye3, wm[...], HIGHEST)
    wait_recv(x_3)
    cross = jnp.concatenate([x_out[0], x_out[1]], axis=0) / total
    coef = nn(wm[:p2, :p2], cross[:p2], HIGHEST)
    cg[y] = coef.astype(BF16)
    k = sems(3)
    cg_1 = go([copy(cg.at[y], cg.at[y], k + d - 1, at_y(d)) for d in (1, 2, 3)])
    wait_recv(lows)
    v_1 = cross_pair(nn(pa[...], rlo[...]), v_in, v_r)
    for q in range(2):
        at = slice(q * q4, (q + 1) * q4)
        residual[at, :] = nn(pit[at, :], rg[y]) + nn(pit[at, :], rlo[...])
    v_2 = reduce_ring(v_in, v_r, v_z, sems(3), v_1)
    for q in range(2, 4):
        at = slice(q * q4, (q + 1) * q4)
        residual[at, :] = nn(pit[at, :], rg[y]) + nn(pit[at, :], rlo[...])

    def settle():
        wait_recv(v_3)
        low = jnp.concatenate([v_out[0], v_out[1]], axis=0) / total
        coef = nn(wm[...], cross + low, HIGHEST)
        coefs[...] = coef
        y_hi, y_lo = split(nn(wtm[...], coef, HIGHEST))
        for q in range(4):
            at = slice(q * q4, (q + 1) * q4)
            residual[at, :] = residual[at, :] - (tn(ptf[q], y_hi) + tn(ptf[q], y_lo))

    wait_recv(h_2)
    h_all = part(h_s, z)[...] + h_z[0] + (h_z[1] + h_z[2])
    hn = nt(h_all, wm[:p2, :p2], HIGHEST).astype(BF16)
    first = jnp.where(iota((group, p2), 1) < bl, hn.astype(F32), 0.0).astype(BF16)
    wait_recv(cg_1)
    sums = [None] * 3
    for j in range(4):
        wait_recv(c_2[j])
        c0 = part(c_own, z, j)[...] + c_z[j, 0].astype(F32) + (c_z[j, 1].astype(F32) + c_z[j, 2].astype(F32))
        for i, v in enumerate((c0, c0 - nn(first, cg[j]), c0 - nn(hn, cg[j]))):
            sums[i] = v * v if sums[i] is None else sums[i] + v * v
    own_group = c * 4 + z
    per = group // bl
    rows8, lanes8 = iota((8, 128), 0), iota((8, 128), 1)
    tile = jnp.zeros((8, 128), F32)
    for i in range(3):
        for b in range(per):
            value = jnp.sum(sums[i][b * bl : (b + 1) * bl, :], axis=(0, 1), keepdims=True)
            spot = (rows8 == i) & (lanes8 == lax.rem(own_group, 2) * per + b)
            tile = jnp.where(spot, value, tile)
    sx[x] = tile
    v_3 = reduce_back(v_z, v_out, sems(1), v_2)
    k = sems(3)
    s_1 = go([copy(sx.at[x], sx.at[x], k + d - 1, at_x(d)) for d in (1, 2, 3)])
    settle()
    wait_recv(s_1)
    sg[s] = (sx[0] + sx[1]) + (sx[2] + sx[3])
    ks = sems(1)

    def tell(d, carry):
        copy(sg.at[s], sg.at[s], ks, at_s(d)).start()
        return carry

    lax.fori_loop(1, 8, tell, 0)
    wait_recv(track([Bulk(sg.at[pl.ds(0, 7)], ss.at[ks], rs.at[ks])]))
    out = jnp.zeros((8, 128), F32)
    for i in range(2):
        grp = 2 * x + i
        out = out + sg[lax.rem(grp, 4) * 2 + grp // 4]
    out = jnp.sqrt(out / (bl * 16 * slab) + EPS)
    scores[...] = out[:3, : 2 * per]

    finish()


def local(dims, basis, strain, route, chosen):
    rk, slab, tslab, bl = dims
    nr, q4, sr = 128 * rk, 32 * rk, 8 * rk
    p3, p2 = 3 * bl, 2 * bl
    half, group = 2 * tslab, tslab // 2
    s, t = lax.axis_index("samp"), lax.axis_index("term")

    routes = route.reshape(128, sr)
    goes = routes // nr
    hit = goes == s
    before = jnp.tril(jnp.ones((sr, sr), jnp.bool_), -1)
    rank = jnp.sum(jnp.where(before[None], hit[:, None, :], False), axis=2)
    slot = hit[:, :, None] & (rank[:, :, None] == jnp.arange(rk)[None, None, :])
    sample = jnp.sum(jnp.where(slot, (routes - goes * nr)[:, :, None], 0), axis=1)
    index = sample.reshape(8, 4, 4, rk).transpose(1, 2, 0, 3).reshape(1, nr)
    own = lax.dynamic_index_in_dim(goes, s * 16 + t, 0, keepdims=False)
    same = (own[:, None] == own[None, :]) & before
    place = (own * rk + jnp.sum(same, axis=1)).reshape(1, sr)

    vmem = pl.BlockSpec(memory_space=pltpu.VMEM)
    scratch = [
        ((4, p3, q4), BF16), ((3, p3, q4), BF16), ((p3, q4), BF16), ((3, p3, q4), BF16), ((4, p3, q4), BF16),
        *[((4, 8, 4, 2 * rk, slab // 2), BF16), ((4, 8, 4, 2 * rk, slab // 2), BF16), ((4, 4, 8, 2 * rk, slab // 2), BF16)] * 2,
        ((nr, nr), BF16), ((4 * tslab, nr), BF16),
        ((4, nr, slab), BF16), ((4, q4, slab), BF16), ((nr, slab), BF16), ((p3, nr), BF16),
        ((2, 3, bl, bl), F32), ((3, bl, bl), F32), ((4, 3, bl, bl), F32), ((2, 3, bl, bl), F32),
        *[((2, p3 // 2, slab), F32), ((p3 // 2, slab), F32), ((4, p3 // 2, slab), F32), ((2, p3 // 2, slab), F32)] * 2,
        ((2, half, p2), F32), ((half, p2), F32), ((half, p2), F32), ((3, group, p2), F32),
        ((4, half, slab), F32), ((4, half, slab), BF16), ((4, half, slab), BF16), ((4, half, slab), BF16),
        ((4, 3, group, slab), BF16), ((4, p2, slab), BF16), ((4, 8, 128), F32), ((8, 8, 128), F32),
        ((3, bl, bl), F32), ((p3, p3), F32), ((p3, p3), F32),
    ]
    return pl.pallas_call(
        functools.partial(body, dims),
        out_shape=(
            jax.ShapeDtypeStruct((nr, slab), F32),
            jax.ShapeDtypeStruct((p3, slab), F32),
            jax.ShapeDtypeStruct((3, tslab // bl), F32),
        ),
        in_specs=[pl.BlockSpec(memory_space=pltpu.SMEM), vmem, vmem, vmem, vmem],
        out_specs=(vmem, vmem, vmem),
        scratch_shapes=[pltpu.VMEM(shape, dtype) for shape, dtype in scratch]
        + [pltpu.SemaphoreType.DMA((128,)), pltpu.SemaphoreType.DMA((128,))],
        compiler_params=pltpu.CompilerParams(
            collective_id=0, has_side_effects=True, vmem_limit_bytes=60 * 1024 * 1024
        ),
    )(chosen, index, place, basis, strain)


def solution(mesh, dims=(8, 256, 256, BLOCK)):
    return jax.shard_map(
        functools.partial(local, dims),
        mesh=mesh,
        in_specs=(P("samp", "term"), P(("samp", "term"), None), P(), P()),
        out_specs=(P("samp", "term"), P(None, "term"), P(None, "term")),
        check_vma=False,
    )
```

```python
import functools

import jax
import jax.numpy as jnp
from jax import lax
from jax.experimental import pallas as pl
from jax.experimental.pallas import tpu as pltpu
from jax.sharding import PartitionSpec as P

BLOCK = 64
STEPS = 3
EPS = 1e-06
MESH = pl.DeviceIdType.MESH
HIGHEST = lax.Precision.HIGHEST
F32 = jnp.float32
BF16 = jnp.bfloat16


def nn(a, b, precision=None):
    return lax.dot_general(
        a, b, (((1,), (0,)), ((), ())), precision=precision, preferred_element_type=F32
    )


def nt(a, b, precision=None):
    return lax.dot_general(
        a, b, (((1,), (1,)), ((), ())), precision=precision, preferred_element_type=F32
    )


def tn(a, b):
    return lax.dot_general(a, b, (((0,), (0,)), ((), ())), preferred_element_type=F32)


def iota(shape, dim):
    return lax.broadcasted_iota(jnp.int32, shape, dim)


def ones_where(mask):
    return jnp.where(mask, 1.0, 0.0).astype(BF16)


def split(v):
    hi = v.astype(BF16)
    return hi, (v - hi.astype(F32)).astype(BF16)


class Bulk:
    def __init__(self, view, send_sem, recv_sem):
        self.view, self.send_sem, self.recv_sem = view, send_sem, recv_sem

    def wait_send(self):
        pltpu.make_async_copy(self.view, self.view, self.send_sem).wait()

    def wait_recv(self):
        pltpu.make_async_copy(self.view, self.view, self.recv_sem).wait()


def inverse_factor(a, width=8):
    n = a.shape[0]
    width = min(width, n)
    rows, cols = iota((n, n), 0), iota((n, n), 1)
    inv = jnp.where(rows == cols, 1.0, 0.0).astype(F32)
    for g in range(0, n, width):
        picked = range(g, g + width)
        columns = [jnp.broadcast_to(a[:, j : j + 1], (n, n)) for j in picked]
        rows_a = [a[j : j + 1, :] for j in picked]
        rows_i = [inv[j : j + 1, :] for j in picked]
        drop_a = drop_i = 0.0
        for i, j in enumerate(picked):
            scale = 1.0 / columns[i][j : j + 1, :]
            unit_a, unit_i = rows_a[i] * scale, rows_i[i] * scale
            below = jnp.where(rows > j, columns[i], 0.0)
            for m in range(i + 1, width):
                factor = columns[i][g + m : g + m + 1, :]
                rows_a[m] = rows_a[m] - factor * unit_a
                rows_i[m] = rows_i[m] - factor * unit_i
                columns[m] = columns[m] - below * (columns[m][j : j + 1, :] * scale)
            drop_a, drop_i = drop_a + below * unit_a, drop_i + below * unit_i
        a, inv = a - drop_a, inv - drop_i
    diag = jnp.sum(jnp.where(rows == cols, a, 0.0), axis=1, keepdims=True)
    return inv / jnp.sqrt(diag)


def body(
    dims, chosen, index, place, basis, strain, residual, coefs, scores,
    ptp, prs, psum, pry, ptf, out_h, mid_h, in_h, out_l, mid_l, in_l, pit, btg, rg, lo, rlo, pa,
    g_in, g_r, g_z, g_out, x_in, x_r, x_z, x_out, v_in, v_r, v_z, v_out, h_in, h_r, h_s, h_z,
    c_own, c_send, c_r, c_s, c_z, cg, sx, sg, wi, wm, wtm, ss, rs,
):
    rk, slab, tslab, bl = dims
    nr, q4, sr = 128 * rk, 32 * rk, 8 * rk
    p3, p2 = 3 * bl, 2 * bl
    half, group, wide = 2 * tslab, tslab // 2, slab // 2
    total = 8 * nr
    s, t = lax.axis_index("samp"), lax.axis_index("term")
    z, c = s // 2, lax.rem(s, 2)
    y, x = t // 4, lax.rem(t, 4)

    def at_x(d):
        return (s, y * 4 + lax.rem(x + d, 4))

    def at_y(d):
        return (s, lax.rem(y + d, 4) * 4 + x)

    def at_s(d):
        return (lax.rem(s + d, 8), t)

    def at_z(d):
        return (lax.rem(z + d, 4) * 2 + c, t)

    partner = (z * 2 + 1 - c, t)

    used = [0]

    def sems(n):
        used[0] += n
        return used[0] - n

    def copy(src, dst, k, dev):
        return pltpu.make_async_remote_copy(
            src_ref=src, dst_ref=dst, send_sem=ss.at[k], recv_sem=rs.at[k],
            device_id=dev, device_id_type=MESH,
        )

    def start(copies):
        for one in copies:
            one.start()
        return copies

    pending, awaited = [], []

    def wait_recv(copies):
        for one in copies:
            one.wait_recv()
            awaited[:] = [other for other in awaited if other is not one]

    def track(copies):
        pending.extend(copies)
        awaited.extend(copies)
        return copies

    def go(copies):
        return start(track(copies))

    def finish():
        wait_recv(list(awaited))
        for one in pending:
            one.wait_send()

    barrier = pltpu.get_barrier_semaphore()

    def greet(dev):
        pl.semaphore_signal(barrier, inc=1, device_id=dev, device_id_type=MESH)

    for d in (1, 2, 3):
        greet(at_x(d))
        greet(at_y(d))
    for d in range(1, 8):
        greet(at_s(d))

    rows = iota((p3, tslab), 0)
    which = jnp.where(rows < bl, chosen[0], jnp.where(rows < p2, chosen[1], chosen[2]))
    target = which * bl + lax.rem(rows, bl) - t * tslab
    select = ones_where(iota((p3, tslab), 1) == target)
    for q in range(4):
        ptp[q] = nt(select, basis[q * q4 : (q + 1) * q4, :]).astype(BF16)

    order = ones_where(iota((sr, sr), 0) == place[...])

    def packed(v):
        pair = [v[:, n * wide : (n + 1) * wide].reshape(8, rk, wide) for n in (0, 1)]
        return jnp.stack(pair, axis=1).reshape(8, 2 * rk, wide).astype(BF16)

    def unpacked(v):
        v = v.astype(F32).reshape(32, 2, rk, wide)
        return jnp.concatenate([v[:, n].reshape(q4, wide) for n in (0, 1)], axis=1).astype(BF16)

    def sort_slab(j, carry):
        for k in range(4):
            at = pl.multiple_of((j * 4 + k) * slab, slab)
            hi, low = split(strain[:, pl.ds(at, slab)])
            out_h[j, :, k] = packed(nn(order, hi))
            out_l[j, :, k] = packed(nn(order, low))
        return carry

    lax.fori_loop(0, 4, sort_slab, 0)

    pl.semaphore_wait(barrier, 13)

    k = sems(3)
    p_1 = go([copy(ptp.at[lax.rem(y + d, 4)], prs.at[d - 1], k + d - 1, at_y(d)) for d in (1, 2, 3)])

    to_s, to_x = {}, {}

    def send_z(low, j):
        src, dst = ((out_h, mid_h), (out_l, mid_l))[low]
        k = sems(1)

        def scatter(d, carry):
            dev = at_s(d)
            copy(src.at[j, dev[0]], dst.at[j, s], k, dev).start()
            return carry

        lax.fori_loop(1, 8, scatter, 0)
        to_s[low, j] = track([Bulk(dst.at[j, pl.ds(0, 7)], ss.at[k], rs.at[k])])
        dst[j, s] = src[j, s]

    def send_x(low, j):
        src, dst = ((mid_h, in_h), (mid_l, in_l))[low]
        wait_recv(to_s[low, j])
        k = sems(3)
        to_x[low, j] = go([copy(src.at[j, :, lax.rem(x + d, 4)], dst.at[j, x], k + d - 1, at_x(d)) for d in (1, 2, 3)])
        dst[j, x] = src[j, :, x]

    send_z(0, 0)
    send_z(0, 1)

    def build(q, carry):
        at = pl.multiple_of(q * q4, q4)
        pit[pl.ds(at, q4), :] = ones_where(iota((q4, nr), 0) + at == index[...])
        return carry

    lax.fori_loop(0, 4, build, 0)
    eye = ones_where(iota((tslab, tslab), 0) == iota((tslab, tslab), 1))
    bt = nt(eye, basis[...]).astype(BF16)
    btg[pl.ds(pl.multiple_of(x * tslab, tslab), tslab), :] = nn(bt, pit[...]).astype(BF16)

    own_rows = pl.ds(pl.multiple_of(y * q4, q4), q4)
    piece = tslab // 4
    b_out, b_on, r_out, r_on = [], [], [], []

    def b_view(slot, i):
        return btg.at[pl.ds(pl.multiple_of(slot * tslab + i * piece, piece), piece), :]

    def r_view(slot, j):
        return rg.at[j, pl.ds(pl.multiple_of(slot * q4, q4), q4), :]

    def ring_out(view, i, at, dev):
        k = sems(2)
        return go([copy(view(at, i), view(at, i), k + n, dev(1 + 2 * n)) for n in (0, 1)])

    def ring_on(view, i, at, dev, out):
        wait_recv([out[i // 2]])
        slot = lax.rem(at + (3, 1)[i // 2], 4)
        k = sems(1)
        return go([copy(view(slot, i), view(slot, i), k, dev((1, 3)[i // 2]))])

    def send_b(i):
        b_out.append(ring_out(b_view, i, x, at_x))

    def pass_b(i):
        b_on.append(ring_on(b_view, i, x, at_x, b_out[i]))

    def send_r(j):
        wait_recv(to_x[0, j])
        rg[j, own_rows, :] = unpacked(in_h[j])
        r_out.append(ring_out(r_view, j, y, at_y))

    def pass_r(j):
        r_on.append(ring_on(r_view, j, y, at_y, r_out[j]))

    send_b(0)
    send_x(0, 0)
    send_z(0, 2)
    wait_recv(p_1)
    psum[...] = ptp[y] + prs[0] + (prs[1] + prs[2])
    k = sems(3)
    p_2 = go([copy(psum, pry.at[d - 1], k + d - 1, at_x(d)) for d in (1, 2, 3)])
    send_b(1)
    send_x(0, 1)
    send_z(0, 3)
    send_r(0)
    pass_b(0)
    wait_recv(p_2)
    ptf[y] = psum[...] + pry[0] + (pry[1] + pry[2])
    k = sems(3)
    p_3 = go([copy(ptf.at[y], ptf.at[y], k + d - 1, at_y(d)) for d in (1, 2, 3)])
    send_x(0, 2)
    send_z(1, 0)
    send_b(2)
    send_r(1)
    pass_r(0)
    pass_b(1)
    send_x(0, 3)
    send_z(1, 1)
    send_b(3)

    def reduce_pair(src, got, k):
        return go([copy(src.at[1 - c], got, k, partner)])

    def reduce_ring(src, got, parts, k, pair):
        wait_recv(pair)
        parts[z] = (src[c].astype(F32) + got[...].astype(F32)).astype(parts.dtype)
        return go([copy(parts.at[z], parts.at[z], k + d - 1, at_z(d)) for d in (1, 2, 3)])

    def reduce_back(parts, out, k, around):
        wait_recv(around)
        four = [parts[n].astype(F32) for n in range(4)]
        out[c] = ((four[0] + four[1]) + (four[2] + four[3])).astype(out.dtype)
        return go([copy(out.at[c], out.at[c], k, partner)])

    wait_recv(p_3)
    at = 0
    for i in range(3):
        for j in range(i + 1):
            acc = None
            for q in range(4):
                one = nt(ptf[q, i * bl : (i + 1) * bl, :], ptf[q, j * bl : (j + 1) * bl, :])
                acc = one if acc is None else acc + one
            g_in[at // 3, at % 3] = acc
            at += 1
    g_1 = reduce_pair(g_in, g_r, sems(1))
    send_r(2)
    pass_r(1)
    pass_b(2)
    g_2 = reduce_ring(g_in, g_r, g_z, sems(3), g_1)
    send_z(1, 2)
    send_z(1, 3)
    acc = None
    for q in range(4):
        one = nn(ptf[q], pit[q * q4 : (q + 1) * q4, :])
        acc = one if acc is None else acc + one
    pa[...] = acc.astype(BF16)
    send_r(3)
    pass_r(2)
    pass_b(3)
    g_3 = reduce_back(g_z, g_out, sems(1), g_2)
    for j in range(4):
        send_x(1, j)
    pass_r(3)

    def lows_on():
        for j in range(4):
            wait_recv(to_x[1, j])
            lo[j] = unpacked(in_l[j])
        k = sems(3)
        rlo[own_rows, :] = lo[y]
        return go([copy(lo.at[lax.rem(y + d, 4)], rlo.at[own_rows, :], k + d - 1, at_y(d)) for d in (1, 2, 3)])

    def left_over(copies):
        return [got for got in copies if any(got is other for other in awaited)]

    def part(ref, zz, *lead):
        return ref.at[(*lead, pl.ds(pl.multiple_of(zz * group, group), group), slice(None))]

    def cross_pair(v, src, got):
        rows = v.shape[0] // 2
        src[0] = v[:rows].astype(src.dtype)
        src[1] = v[rows:].astype(src.dtype)
        return reduce_pair(src, got, sems(1))

    for i in range(4):
        wait_recv(left_over(b_out[i] + b_on[i]))
    other_half = pl.ds(pl.multiple_of((1 - c) * half, half), half)
    own_half = pl.ds(pl.multiple_of(c * half, half), half)
    ck, cz = sems(4), sems(12)
    c_1, c_2 = [], []

    def correlate(j):
        wait_recv(left_over(r_out[j] + r_on[j]))
        c_send[j] = nn(btg[other_half, :], rg[j]).astype(BF16)
        c_1.append(go([copy(c_send.at[j], c_r.at[j], ck + j, partner)]))
        c_own[j] = nn(btg[own_half, :], rg[j])

    def pass_on(j):
        wait_recv(c_1[j])
        both = c_own[j] + c_r[j].astype(F32)
        c_own[j] = both
        c_s[j] = both.astype(BF16)
        c_2.append(
            go([copy(part(c_s, lax.rem(z + d, 4), j), c_z.at[j, d - 1], cz + 3 * j + d - 1, at_z(d)) for d in (1, 2, 3)])
        )

    hk = sems(1)
    h_in[1] = nt(btg[other_half, :], pa[:p2, :]).astype(BF16)
    h_1 = go([copy(h_in.at[1], h_r, hk, partner)])
    h_in[0] = nt(btg[own_half, :], pa[:p2, :]).astype(BF16)
    correlate(0)
    wait_recv(h_1)
    h_s[...] = (h_in[0].astype(F32) + h_r[...].astype(F32)).astype(BF16)
    k = sems(3)
    h_2 = go([copy(part(h_s, lax.rem(z + d, 4)), h_z.at[d - 1], k + d - 1, at_z(d)) for d in (1, 2, 3)])
    for j in range(4):
        wait_recv(left_over(r_out[j] + r_on[j]))
    x_1 = cross_pair(nn(pa[:p2, :], rg[y]), x_in, x_r)
    correlate(1)
    pass_on(0)
    x_2 = reduce_ring(x_in, x_r, x_z, sems(3), x_1)
    lows = lows_on()

    wait_recv(g_3)

    def factor(i, a):
        wi[i] = inverse_factor(a)

    def rest(i, j):
        return g_out[(i * (i + 1) // 2 + j) // 3, (i * (i + 1) // 2 + j) % 3] / total

    factor(0, rest(0, 0))
    w00 = wi[0]
    l10, l20 = nt(rest(1, 0), w00, HIGHEST), nt(rest(2, 0), w00, HIGHEST)
    pass_on(1)
    correlate(2)
    x_3 = reduce_back(x_z, x_out, sems(1), x_2)
    factor(1, rest(1, 1) - nt(l10, l10, HIGHEST))
    pass_on(2)
    correlate(3)
    w11 = wi[1]
    l21 = nt(rest(2, 1) - nt(l20, l10, HIGHEST), w11, HIGHEST)
    factor(2, rest(2, 2) - nt(l20, l20, HIGHEST) - nt(l21, l21, HIGHEST))
    pass_on(3)
    wait_recv(lows)
    v_1 = cross_pair(nn(pa[...], rg[y]) + nn(pa[...], rlo[...]), v_in, v_r)
    w22 = wi[2]
    w10 = -nn(w11, nn(l10, w00, HIGHEST), HIGHEST)
    w20 = -nn(w22, nn(l20, w00, HIGHEST) + nn(l21, w10, HIGHEST), HIGHEST)
    w21 = -nn(w22, nn(l21, w11, HIGHEST), HIGHEST)
    zero = jnp.zeros((bl, bl), F32)
    wm[...] = jnp.concatenate(
        [
            jnp.concatenate([w00, zero, zero], axis=1),
            jnp.concatenate([w10, w11, zero], axis=1),
            jnp.concatenate([w20, w21, w22], axis=1),
        ],
        axis=0,
    )
    eye3 = jnp.where(iota((p3, p3), 0) == iota((p3, p3), 1), 1.0, 0.0).astype(F32)
    wtm[...] = nt(eye3, wm[...], HIGHEST)
    wait_recv(x_3)
    cross = jnp.concatenate([x_out[0], x_out[1]], axis=0).astype(F32) / total
    coef = nn(wm[:p2, :p2], cross, HIGHEST)
    cg[y] = coef.astype(BF16)
    k = sems(3)
    cg_1 = go([copy(cg.at[y], cg.at[y], k + d - 1, at_y(d)) for d in (1, 2, 3)])
    v_2 = reduce_ring(v_in, v_r, v_z, sems(3), v_1)
    for q in range(4):
        at = slice(q * q4, (q + 1) * q4)
        residual[at, :] = nn(pit[at, :], rg[y]) + nn(pit[at, :], rlo[...])

    def settle():
        wait_recv(v_3)
        full = jnp.concatenate([v_out[0], v_out[1]], axis=0) / total
        coef = nn(wm[...], full, HIGHEST)
        coefs[...] = coef
        y_hi, y_lo = split(nn(wtm[...], coef, HIGHEST))
        for q in range(4):
            at = slice(q * q4, (q + 1) * q4)
            residual[at, :] = residual[at, :] - (tn(ptf[q], y_hi) + tn(ptf[q], y_lo))

    wait_recv(h_2)
    four = [v.astype(F32) for v in (part(h_s, z)[...], h_z[0], h_z[1], h_z[2])]
    h_all = (four[0] + four[1]) + (four[2] + four[3])
    hn = nt(h_all, wm[:p2, :p2], HIGHEST).astype(BF16)
    first = jnp.where(iota((group, p2), 1) < bl, hn.astype(F32), 0.0).astype(BF16)
    wait_recv(cg_1)
    sums = [None] * 3
    for j in range(4):
        wait_recv(c_2[j])
        c0 = part(c_own, z, j)[...] + c_z[j, 0].astype(F32) + (c_z[j, 1].astype(F32) + c_z[j, 2].astype(F32))
        for i, v in enumerate((c0, c0 - nn(first, cg[j]), c0 - nn(hn, cg[j]))):
            sums[i] = v * v if sums[i] is None else sums[i] + v * v
    own_group = c * 4 + z
    per = group // bl
    rows8, lanes8 = iota((8, 128), 0), iota((8, 128), 1)
    tile = jnp.zeros((8, 128), F32)
    for i in range(3):
        for b in range(per):
            value = jnp.sum(sums[i][b * bl : (b + 1) * bl, :], axis=(0, 1), keepdims=True)
            spot = (rows8 == i) & (lanes8 == lax.rem(own_group, 2) * per + b)
            tile = jnp.where(spot, value, tile)
    sx[x] = tile
    v_3 = reduce_back(v_z, v_out, sems(1), v_2)
    k = sems(3)
    s_1 = go([copy(sx.at[x], sx.at[x], k + d - 1, at_x(d)) for d in (1, 2, 3)])
    wait_recv(s_1)
    sg[s] = (sx[0] + sx[1]) + (sx[2] + sx[3])
    ks = sems(1)

    def tell(d, carry):
        copy(sg.at[s], sg.at[s], ks, at_s(d)).start()
        return carry

    lax.fori_loop(1, 8, tell, 0)
    settle()
    wait_recv(track([Bulk(sg.at[pl.ds(0, 7)], ss.at[ks], rs.at[ks])]))
    out = jnp.zeros((8, 128), F32)
    for i in range(2):
        grp = 2 * x + i
        out = out + sg[lax.rem(grp, 4) * 2 + grp // 4]
    out = jnp.sqrt(out / (bl * 16 * slab) + EPS)
    scores[...] = out[:3, : 2 * per]

    finish()


def local(dims, basis, strain, route, chosen):
    rk, slab, tslab, bl = dims
    nr, q4, sr = 128 * rk, 32 * rk, 8 * rk
    p3, p2 = 3 * bl, 2 * bl
    half, group = 2 * tslab, tslab // 2
    s, t = lax.axis_index("samp"), lax.axis_index("term")

    routes = route.reshape(128, sr)
    goes = routes // nr
    hit = goes == s
    before = jnp.tril(jnp.ones((sr, sr), jnp.bool_), -1)
    rank = jnp.sum(jnp.where(before[None], hit[:, None, :], False), axis=2)
    slot = hit[:, :, None] & (rank[:, :, None] == jnp.arange(rk)[None, None, :])
    sample = jnp.sum(jnp.where(slot, (routes - goes * nr)[:, :, None], 0), axis=1)
    index = sample.reshape(8, 4, 4, rk).transpose(1, 2, 0, 3).reshape(1, nr)
    own = lax.dynamic_index_in_dim(goes, s * 16 + t, 0, keepdims=False)
    same = (own[:, None] == own[None, :]) & before
    place = (own * rk + jnp.sum(same, axis=1)).reshape(1, sr)

    vmem = pl.BlockSpec(memory_space=pltpu.VMEM)
    scratch = [
        ((4, p3, q4), BF16), ((3, p3, q4), BF16), ((p3, q4), BF16), ((3, p3, q4), BF16), ((4, p3, q4), BF16),
        *[((4, 8, 4, 2 * rk, slab // 2), BF16), ((4, 8, 4, 2 * rk, slab // 2), BF16), ((4, 4, 8, 2 * rk, slab // 2), BF16)] * 2,
        ((nr, nr), BF16), ((4 * tslab, nr), BF16),
        ((4, nr, slab), BF16), ((4, q4, slab), BF16), ((nr, slab), BF16), ((p3, nr), BF16),
        ((2, 3, bl, bl), F32), ((3, bl, bl), F32), ((4, 3, bl, bl), F32), ((2, 3, bl, bl), F32),
        ((2, bl, slab), BF16), ((bl, slab), BF16), ((4, bl, slab), BF16), ((2, bl, slab), BF16),
        ((2, p3 // 2, slab), F32), ((p3 // 2, slab), F32), ((4, p3 // 2, slab), F32), ((2, p3 // 2, slab), F32),
        ((2, half, p2), BF16), ((half, p2), BF16), ((half, p2), BF16), ((3, group, p2), BF16),
        ((4, half, slab), F32), ((4, half, slab), BF16), ((4, half, slab), BF16), ((4, half, slab), BF16),
        ((4, 3, group, slab), BF16), ((4, p2, slab), BF16), ((4, 8, 128), F32), ((8, 8, 128), F32),
        ((3, bl, bl), F32), ((p3, p3), F32), ((p3, p3), F32),
    ]
    return pl.pallas_call(
        functools.partial(body, dims),
        out_shape=(
            jax.ShapeDtypeStruct((nr, slab), F32),
            jax.ShapeDtypeStruct((p3, slab), F32),
            jax.ShapeDtypeStruct((3, tslab // bl), F32),
        ),
        in_specs=[pl.BlockSpec(memory_space=pltpu.SMEM), vmem, vmem, vmem, vmem],
        out_specs=(vmem, vmem, vmem),
        scratch_shapes=[pltpu.VMEM(shape, dtype) for shape, dtype in scratch]
        + [pltpu.SemaphoreType.DMA((128,)), pltpu.SemaphoreType.DMA((128,))],
        compiler_params=pltpu.CompilerParams(
            collective_id=0, has_side_effects=True, vmem_limit_bytes=60 * 1024 * 1024
        ),
    )(chosen, index, place, basis, strain)


def solution(mesh, dims=(8, 256, 256, BLOCK)):
    return jax.shard_map(
        functools.partial(local, dims),
        mesh=mesh,
        in_specs=(P("samp", "term"), P(("samp", "term"), None), P(), P()),
        out_specs=(P("samp", "term"), P(None, "term"), P(None, "term")),
        check_vma=False,
    )
```

```python
import functools

import jax
import jax.numpy as jnp
from jax import lax
from jax.experimental import pallas as pl
from jax.experimental.pallas import tpu as pltpu
from jax.sharding import PartitionSpec as P

BLOCK = 64
STEPS = 3
EPS = 1e-06
MESH = pl.DeviceIdType.MESH
HIGHEST = lax.Precision.HIGHEST
F32 = jnp.float32
BF16 = jnp.bfloat16


def nn(a, b, precision=None):
    return lax.dot_general(
        a, b, (((1,), (0,)), ((), ())), precision=precision, preferred_element_type=F32
    )


def nt(a, b, precision=None):
    return lax.dot_general(
        a, b, (((1,), (1,)), ((), ())), precision=precision, preferred_element_type=F32
    )


def tn(a, b):
    return lax.dot_general(a, b, (((0,), (0,)), ((), ())), preferred_element_type=F32)


def iota(shape, dim):
    return lax.broadcasted_iota(jnp.int32, shape, dim)


def ones_where(mask):
    return jnp.where(mask, 1.0, 0.0).astype(BF16)


def split(v):
    hi = v.astype(BF16)
    return hi, (v - hi.astype(F32)).astype(BF16)


class Bulk:
    def __init__(self, view, send_sem, recv_sem):
        self.view, self.send_sem, self.recv_sem = view, send_sem, recv_sem

    def wait_send(self):
        pltpu.make_async_copy(self.view, self.view, self.send_sem).wait()

    def wait_recv(self):
        pltpu.make_async_copy(self.view, self.view, self.recv_sem).wait()


def inverse_factor(a, width=8):
    n = a.shape[0]
    width = min(width, n)
    rows, cols = iota((n, n), 0), iota((n, n), 1)
    inv = jnp.where(rows == cols, 1.0, 0.0).astype(F32)
    for g in range(0, n, width):
        picked = range(g, g + width)
        columns = [jnp.broadcast_to(a[:, j : j + 1], (n, n)) for j in picked]
        rows_a = [a[j : j + 1, :] for j in picked]
        rows_i = [inv[j : j + 1, :] for j in picked]
        drop_a = drop_i = 0.0
        for i, j in enumerate(picked):
            scale = 1.0 / columns[i][j : j + 1, :]
            unit_a, unit_i = rows_a[i] * scale, rows_i[i] * scale
            below = jnp.where(rows > j, columns[i], 0.0)
            for m in range(i + 1, width):
                factor = columns[i][g + m : g + m + 1, :]
                rows_a[m] = rows_a[m] - factor * unit_a
                rows_i[m] = rows_i[m] - factor * unit_i
                columns[m] = columns[m] - below * (columns[m][j : j + 1, :] * scale)
            drop_a, drop_i = drop_a + below * unit_a, drop_i + below * unit_i
        a, inv = a - drop_a, inv - drop_i
    diag = jnp.sum(jnp.where(rows == cols, a, 0.0), axis=1, keepdims=True)
    return inv / jnp.sqrt(diag)


def body(
    dims, chosen, route, basis, strain, residual, coefs, scores,
    ptp, prs, psum, pry, ptf, out_h, mid_h, in_h, out_l, mid_l, in_l, pit, btg, rg, lo, rlo, pa,
    g_in, g_r, g_z, g_out, x_in, x_r, x_z, x_out, v_in, v_r, v_z, v_out, h_in, h_r, h_s, h_z,
    c_own, c_send, c_r, c_s, c_z, cg, sx, sg, wi, wm, wtm, index, ss, rs,
):
    rk, slab, tslab, bl = dims
    nr, q4, sr = 128 * rk, 32 * rk, 8 * rk
    p3, p2 = 3 * bl, 2 * bl
    half, group, wide = 2 * tslab, tslab // 2, slab // 2
    total = 8 * nr
    s, t = lax.axis_index("samp"), lax.axis_index("term")
    z, c = s // 2, lax.rem(s, 2)
    y, x = t // 4, lax.rem(t, 4)

    def at_x(d):
        return (s, y * 4 + lax.rem(x + d, 4))

    def at_y(d):
        return (s, lax.rem(y + d, 4) * 4 + x)

    def at_s(d):
        return (lax.rem(s + d, 8), t)

    def at_z(d):
        return (lax.rem(z + d, 4) * 2 + c, t)

    partner = (z * 2 + 1 - c, t)

    used = [0]

    def sems(n):
        used[0] += n
        return used[0] - n

    def copy(src, dst, k, dev):
        return pltpu.make_async_remote_copy(
            src_ref=src, dst_ref=dst, send_sem=ss.at[k], recv_sem=rs.at[k],
            device_id=dev, device_id_type=MESH,
        )

    def start(copies):
        for one in copies:
            one.start()
        return copies

    pending, awaited = [], []

    def wait_recv(copies):
        for one in copies:
            one.wait_recv()
            awaited[:] = [other for other in awaited if other is not one]

    def track(copies):
        pending.extend(copies)
        awaited.extend(copies)
        return copies

    def go(copies):
        return start(track(copies))

    def finish():
        wait_recv(list(awaited))
        for one in pending:
            one.wait_send()

    barrier = pltpu.get_barrier_semaphore()

    def greet(dev):
        pl.semaphore_signal(barrier, inc=1, device_id=dev, device_id_type=MESH)

    for d in (1, 2, 3):
        greet(at_x(d))
        greet(at_y(d))
    for d in range(1, 8):
        greet(at_s(d))

    rows = iota((p3, tslab), 0)
    which = jnp.where(rows < bl, chosen[0], jnp.where(rows < p2, chosen[1], chosen[2]))
    target = which * bl + lax.rem(rows, bl) - t * tslab
    select = ones_where(iota((p3, tslab), 1) == target)
    for q in range(4):
        ptp[q] = nt(select, basis[q * q4 : (q + 1) * q4, :]).astype(BF16)

    bits, fold = nr.bit_length() - 1, 5
    ahead = ones_where(
        (iota((2 * sr, 2 * sr), 0) < iota((2 * sr, 2 * sr), 1))
        & ((iota((2 * sr, 2 * sr), 0) >= sr) == (iota((2 * sr, 2 * sr), 1) >= sr))
    )
    own = route[pl.ds(s * 8 + t // 2, 1), :]
    own = jnp.where(lax.rem(t, 2) == 1, own[:, sr:], own[:, :sr]) >> bits
    to = iota((8, sr), 0) == own
    place = nn(ones_where(to), ahead[:sr, :sr]) + (iota((8, sr), 0) * rk).astype(F32)
    place = jnp.sum(jnp.where(to, place, 0.0), axis=0, keepdims=True)
    order = ones_where(iota((sr, sr), 0).astype(F32) == place)

    def packed(v):
        pair = [v[:, n * wide : (n + 1) * wide].reshape(8, rk, wide) for n in (0, 1)]
        return jnp.stack(pair, axis=1).reshape(8, 2 * rk, wide).astype(BF16)

    def unpacked(v):
        v = v.astype(F32).reshape(32, 2, rk, wide)
        return jnp.concatenate([v[:, n].reshape(q4, wide) for n in (0, 1)], axis=1).astype(BF16)

    def sort_slab(j, carry):
        for k in range(4):
            at = pl.multiple_of((j * 4 + k) * slab, slab)
            hi, low = split(strain[:, pl.ds(at, slab)])
            out_h[j, :, k] = packed(nn(order, hi))
            out_l[j, :, k] = packed(nn(order, low))
        return carry

    lax.fori_loop(0, 4, sort_slab, 0)

    hit = (route[...] >> bits) == s
    code = jnp.where(hit, nn(ones_where(hit), ahead) + 1.0, 0.0).astype(BF16)
    spot = route[...] & (nr - 1)
    high, low = (spot >> fold).astype(F32).astype(BF16), (spot & ((1 << fold) - 1)).astype(F32).astype(BF16)
    at = iota((q4, 64), 0)
    px, ps = at // sr, lax.rem(at // rk, 8)
    back = iota((q4, 2 * sr), 0)
    half_of = lax.rem(back // sr, 2) == (iota((q4, 2 * sr), 1) >= sr).astype(jnp.int32)
    turn = (lax.rem(back, rk) + 1).astype(F32)
    every = jnp.ones((8, 2 * sr), BF16)
    for q in range(4):
        pick = ones_where(iota((q4, 64), 1) == ps * 8 + q * 2 + px // 2)
        here = half_of & (nn(pick, code) == turn)
        big = nt(every, jnp.where(here, nn(pick, high), 0.0).astype(BF16))
        small = nt(every, jnp.where(here, nn(pick, low), 0.0).astype(BF16))
        index[:, q * q4 : (q + 1) * q4] = (big[:1] * (1 << fold) + small[:1]).astype(jnp.int32)

    pl.semaphore_wait(barrier, 13)

    k = sems(3)
    p_1 = go([copy(ptp.at[lax.rem(y + d, 4)], prs.at[d - 1], k + d - 1, at_y(d)) for d in (1, 2, 3)])

    to_s, to_x = {}, {}

    def send_z(low, j):
        src, dst = ((out_h, mid_h), (out_l, mid_l))[low]
        k = sems(1)

        def scatter(d, carry):
            dev = at_s(d)
            copy(src.at[j, dev[0]], dst.at[j, s], k, dev).start()
            return carry

        lax.fori_loop(1, 8, scatter, 0)
        to_s[low, j] = track([Bulk(dst.at[j, pl.ds(0, 7)], ss.at[k], rs.at[k])])
        dst[j, s] = src[j, s]

    def send_x(low, j):
        src, dst = ((mid_h, in_h), (mid_l, in_l))[low]
        wait_recv(to_s[low, j])
        k = sems(3)
        to_x[low, j] = go([copy(src.at[j, :, lax.rem(x + d, 4)], dst.at[j, x], k + d - 1, at_x(d)) for d in (1, 2, 3)])
        dst[j, x] = src[j, :, x]

    send_z(0, 0)
    send_z(0, 1)

    def build(q, carry):
        at = pl.multiple_of(q * q4, q4)
        pit[pl.ds(at, q4), :] = ones_where(iota((q4, nr), 0) + at == index[...])
        return carry

    lax.fori_loop(0, 4, build, 0)
    eye = ones_where(iota((tslab, tslab), 0) == iota((tslab, tslab), 1))
    bt = nt(eye, basis[...]).astype(BF16)
    btg[pl.ds(pl.multiple_of(x * tslab, tslab), tslab), :] = nn(bt, pit[...]).astype(BF16)

    own_rows = pl.ds(pl.multiple_of(y * q4, q4), q4)
    piece = tslab // 4
    b_out, b_on, r_out, r_on = [], [], [], []

    def b_view(slot, i):
        return btg.at[pl.ds(pl.multiple_of(slot * tslab + i * piece, piece), piece), :]

    def r_view(slot, j):
        return rg.at[j, pl.ds(pl.multiple_of(slot * q4, q4), q4), :]

    def ring_out(view, i, at, dev):
        k = sems(2)
        return go([copy(view(at, i), view(at, i), k + n, dev(1 + 2 * n)) for n in (0, 1)])

    def ring_on(view, i, at, dev, out):
        wait_recv([out[i // 2]])
        slot = lax.rem(at + (3, 1)[i // 2], 4)
        k = sems(1)
        return go([copy(view(slot, i), view(slot, i), k, dev((1, 3)[i // 2]))])

    def send_b(i):
        b_out.append(ring_out(b_view, i, x, at_x))

    def pass_b(i):
        b_on.append(ring_on(b_view, i, x, at_x, b_out[i]))

    def send_r(j):
        wait_recv(to_x[0, j])
        rg[j, own_rows, :] = unpacked(in_h[j])
        r_out.append(ring_out(r_view, j, y, at_y))

    def pass_r(j):
        r_on.append(ring_on(r_view, j, y, at_y, r_out[j]))

    send_b(0)
    send_x(0, 0)
    send_z(0, 2)
    wait_recv(p_1)
    psum[...] = ptp[y] + prs[0] + (prs[1] + prs[2])
    k = sems(3)
    p_2 = go([copy(psum, pry.at[d - 1], k + d - 1, at_x(d)) for d in (1, 2, 3)])
    send_b(1)
    send_x(0, 1)
    send_z(0, 3)
    send_r(0)
    pass_b(0)
    wait_recv(p_2)
    ptf[y] = psum[...] + pry[0] + (pry[1] + pry[2])
    k = sems(3)
    p_3 = go([copy(ptf.at[y], ptf.at[y], k + d - 1, at_y(d)) for d in (1, 2, 3)])
    send_x(0, 2)
    send_z(1, 0)
    send_b(2)
    send_r(1)
    pass_r(0)
    pass_b(1)
    send_x(0, 3)
    send_z(1, 1)
    send_b(3)

    def reduce_pair(src, got, k):
        return go([copy(src.at[1 - c], got, k, partner)])

    def reduce_ring(src, got, parts, k, pair):
        wait_recv(pair)
        parts[z] = (src[c].astype(F32) + got[...].astype(F32)).astype(parts.dtype)
        return go([copy(parts.at[z], parts.at[z], k + d - 1, at_z(d)) for d in (1, 2, 3)])

    def reduce_back(parts, out, k, around):
        wait_recv(around)
        four = [parts[n].astype(F32) for n in range(4)]
        out[c] = ((four[0] + four[1]) + (four[2] + four[3])).astype(out.dtype)
        return go([copy(out.at[c], out.at[c], k, partner)])

    wait_recv(p_3)
    at = 0
    for i in range(3):
        for j in range(i + 1):
            acc = None
            for q in range(4):
                one = nt(ptf[q, i * bl : (i + 1) * bl, :], ptf[q, j * bl : (j + 1) * bl, :])
                acc = one if acc is None else acc + one
            g_in[at // 3, at % 3] = acc
            at += 1
    g_1 = reduce_pair(g_in, g_r, sems(1))
    send_r(2)
    pass_r(1)
    pass_b(2)
    g_2 = reduce_ring(g_in, g_r, g_z, sems(3), g_1)
    send_z(1, 2)
    send_z(1, 3)
    acc = None
    for q in range(4):
        one = nn(ptf[q], pit[q * q4 : (q + 1) * q4, :])
        acc = one if acc is None else acc + one
    pa[...] = acc.astype(BF16)
    send_r(3)
    pass_r(2)
    pass_b(3)
    g_3 = reduce_back(g_z, g_out, sems(1), g_2)
    for j in range(4):
        send_x(1, j)
    pass_r(3)

    def lows_on():
        for j in range(4):
            wait_recv(to_x[1, j])
            lo[j] = unpacked(in_l[j])
        k = sems(3)
        rlo[own_rows, :] = lo[y]
        return go([copy(lo.at[lax.rem(y + d, 4)], rlo.at[own_rows, :], k + d - 1, at_y(d)) for d in (1, 2, 3)])

    def left_over(copies):
        return [got for got in copies if any(got is other for other in awaited)]

    def part(ref, zz, *lead):
        return ref.at[(*lead, pl.ds(pl.multiple_of(zz * group, group), group), slice(None))]

    def cross_pair(v, src, got):
        rows = v.shape[0] // 2
        src[0] = v[:rows].astype(src.dtype)
        src[1] = v[rows:].astype(src.dtype)
        return reduce_pair(src, got, sems(1))

    for i in range(4):
        wait_recv(left_over(b_out[i] + b_on[i]))
    other_half = pl.ds(pl.multiple_of((1 - c) * half, half), half)
    own_half = pl.ds(pl.multiple_of(c * half, half), half)
    ck, cz = sems(4), sems(12)
    c_1, c_2 = [], []

    def correlate(j):
        wait_recv(left_over(r_out[j] + r_on[j]))
        c_send[j] = nn(btg[other_half, :], rg[j]).astype(BF16)
        c_1.append(go([copy(c_send.at[j], c_r.at[j], ck + j, partner)]))
        c_own[j] = nn(btg[own_half, :], rg[j])

    def pass_on(j):
        wait_recv(c_1[j])
        both = c_own[j] + c_r[j].astype(F32)
        c_own[j] = both
        c_s[j] = both.astype(BF16)
        c_2.append(
            go([copy(part(c_s, lax.rem(z + d, 4), j), c_z.at[j, d - 1], cz + 3 * j + d - 1, at_z(d)) for d in (1, 2, 3)])
        )

    hk = sems(1)
    h_in[1] = nt(btg[other_half, :], pa[:p2, :]).astype(BF16)
    h_1 = go([copy(h_in.at[1], h_r, hk, partner)])
    h_in[0] = nt(btg[own_half, :], pa[:p2, :]).astype(BF16)
    correlate(0)
    wait_recv(h_1)
    h_s[...] = (h_in[0].astype(F32) + h_r[...].astype(F32)).astype(BF16)
    k = sems(3)
    h_2 = go([copy(part(h_s, lax.rem(z + d, 4)), h_z.at[d - 1], k + d - 1, at_z(d)) for d in (1, 2, 3)])
    for j in range(4):
        wait_recv(left_over(r_out[j] + r_on[j]))
    x_1 = cross_pair(nn(pa[:p2, :], rg[y]), x_in, x_r)
    correlate(1)
    pass_on(0)
    x_2 = reduce_ring(x_in, x_r, x_z, sems(3), x_1)
    lows = lows_on()

    wait_recv(g_3)

    def factor(i, a):
        wi[i] = inverse_factor(a)

    def rest(i, j):
        return g_out[(i * (i + 1) // 2 + j) // 3, (i * (i + 1) // 2 + j) % 3] / total

    factor(0, rest(0, 0))
    w00 = wi[0]
    l10, l20 = nt(rest(1, 0), w00, HIGHEST), nt(rest(2, 0), w00, HIGHEST)
    pass_on(1)
    correlate(2)
    x_3 = reduce_back(x_z, x_out, sems(1), x_2)
    factor(1, rest(1, 1) - nt(l10, l10, HIGHEST))
    pass_on(2)
    correlate(3)
    w11 = wi[1]
    l21 = nt(rest(2, 1) - nt(l20, l10, HIGHEST), w11, HIGHEST)
    factor(2, rest(2, 2) - nt(l20, l20, HIGHEST) - nt(l21, l21, HIGHEST))
    pass_on(3)
    wait_recv(lows)
    v_1 = cross_pair(nn(pa[...], rg[y]) + nn(pa[...], rlo[...]), v_in, v_r)
    w22 = wi[2]
    w10 = -nn(w11, nn(l10, w00, HIGHEST), HIGHEST)
    w20 = -nn(w22, nn(l20, w00, HIGHEST) + nn(l21, w10, HIGHEST), HIGHEST)
    w21 = -nn(w22, nn(l21, w11, HIGHEST), HIGHEST)
    zero = jnp.zeros((bl, bl), F32)
    wm[...] = jnp.concatenate(
        [
            jnp.concatenate([w00, zero, zero], axis=1),
            jnp.concatenate([w10, w11, zero], axis=1),
            jnp.concatenate([w20, w21, w22], axis=1),
        ],
        axis=0,
    )
    eye3 = jnp.where(iota((p3, p3), 0) == iota((p3, p3), 1), 1.0, 0.0).astype(F32)
    wtm[...] = nt(eye3, wm[...], HIGHEST)
    wait_recv(x_3)
    cross = jnp.concatenate([x_out[0], x_out[1]], axis=0).astype(F32) / total
    coef = nn(wm[:p2, :p2], cross, HIGHEST)
    cg[y] = coef.astype(BF16)
    k = sems(3)
    cg_1 = go([copy(cg.at[y], cg.at[y], k + d - 1, at_y(d)) for d in (1, 2, 3)])
    v_2 = reduce_ring(v_in, v_r, v_z, sems(3), v_1)
    for q in range(4):
        at = slice(q * q4, (q + 1) * q4)
        residual[at, :] = nn(pit[at, :], rg[y]) + nn(pit[at, :], rlo[...])

    def settle():
        wait_recv(v_3)
        full = jnp.concatenate([v_out[0], v_out[1]], axis=0) / total
        coef = nn(wm[...], full, HIGHEST)
        coefs[...] = coef
        y_hi, y_lo = split(nn(wtm[...], coef, HIGHEST))
        for q in range(4):
            at = slice(q * q4, (q + 1) * q4)
            residual[at, :] = residual[at, :] - (tn(ptf[q], y_hi) + tn(ptf[q], y_lo))

    wait_recv(h_2)
    four = [v.astype(F32) for v in (part(h_s, z)[...], h_z[0], h_z[1], h_z[2])]
    h_all = (four[0] + four[1]) + (four[2] + four[3])
    hn = nt(h_all, wm[:p2, :p2], HIGHEST).astype(BF16)
    first = jnp.where(iota((group, p2), 1) < bl, hn.astype(F32), 0.0).astype(BF16)
    wait_recv(cg_1)
    sums = [None] * 3
    for j in range(4):
        wait_recv(c_2[j])
        c0 = part(c_own, z, j)[...] + c_z[j, 0].astype(F32) + (c_z[j, 1].astype(F32) + c_z[j, 2].astype(F32))
        for i, v in enumerate((c0, c0 - nn(first, cg[j]), c0 - nn(hn, cg[j]))):
            sums[i] = v * v if sums[i] is None else sums[i] + v * v
    own_group = c * 4 + z
    per = group // bl
    rows8, lanes8 = iota((8, 128), 0), iota((8, 128), 1)
    tile = jnp.zeros((8, 128), F32)
    for i in range(3):
        for b in range(per):
            value = jnp.sum(sums[i][b * bl : (b + 1) * bl, :], axis=(0, 1), keepdims=True)
            spot = (rows8 == i) & (lanes8 == lax.rem(own_group, 2) * per + b)
            tile = jnp.where(spot, value, tile)
    sx[x] = tile
    v_3 = reduce_back(v_z, v_out, sems(1), v_2)
    k = sems(3)
    s_1 = go([copy(sx.at[x], sx.at[x], k + d - 1, at_x(d)) for d in (1, 2, 3)])
    wait_recv(s_1)
    sg[s] = (sx[0] + sx[1]) + (sx[2] + sx[3])
    ks = sems(1)

    def tell(d, carry):
        copy(sg.at[s], sg.at[s], ks, at_s(d)).start()
        return carry

    lax.fori_loop(1, 8, tell, 0)
    settle()
    wait_recv(track([Bulk(sg.at[pl.ds(0, 7)], ss.at[ks], rs.at[ks])]))
    out = jnp.zeros((8, 128), F32)
    for i in range(2):
        grp = 2 * x + i
        out = out + sg[lax.rem(grp, 4) * 2 + grp // 4]
    out = jnp.sqrt(out / (bl * 16 * slab) + EPS)
    scores[...] = out[:3, : 2 * per]

    finish()


def local(dims, basis, strain, route, chosen):
    rk, slab, tslab, bl = dims
    nr, q4, sr = 128 * rk, 32 * rk, 8 * rk
    p3, p2 = 3 * bl, 2 * bl
    half, group = 2 * tslab, tslab // 2
    vmem = pl.BlockSpec(memory_space=pltpu.VMEM)
    scratch = [
        ((4, p3, q4), BF16), ((3, p3, q4), BF16), ((p3, q4), BF16), ((3, p3, q4), BF16), ((4, p3, q4), BF16),
        *[((4, 8, 4, 2 * rk, slab // 2), BF16), ((4, 8, 4, 2 * rk, slab // 2), BF16), ((4, 4, 8, 2 * rk, slab // 2), BF16)] * 2,
        ((nr, nr), BF16), ((4 * tslab, nr), BF16),
        ((4, nr, slab), BF16), ((4, q4, slab), BF16), ((nr, slab), BF16), ((p3, nr), BF16),
        ((2, 3, bl, bl), F32), ((3, bl, bl), F32), ((4, 3, bl, bl), F32), ((2, 3, bl, bl), F32),
        ((2, bl, slab), BF16), ((bl, slab), BF16), ((4, bl, slab), BF16), ((2, bl, slab), BF16),
        ((2, p3 // 2, slab), F32), ((p3 // 2, slab), F32), ((4, p3 // 2, slab), F32), ((2, p3 // 2, slab), F32),
        ((2, half, p2), BF16), ((half, p2), BF16), ((half, p2), BF16), ((3, group, p2), BF16),
        ((4, half, slab), F32), ((4, half, slab), BF16), ((4, half, slab), BF16), ((4, half, slab), BF16),
        ((4, 3, group, slab), BF16), ((4, p2, slab), BF16), ((4, 8, 128), F32), ((8, 8, 128), F32),
        ((3, bl, bl), F32), ((p3, p3), F32), ((p3, p3), F32), ((1, nr), jnp.int32),
    ]
    return pl.pallas_call(
        functools.partial(body, dims),
        out_shape=(
            jax.ShapeDtypeStruct((nr, slab), F32),
            jax.ShapeDtypeStruct((p3, slab), F32),
            jax.ShapeDtypeStruct((3, tslab // bl), F32),
        ),
        in_specs=[pl.BlockSpec(memory_space=pltpu.SMEM), vmem, vmem, vmem],
        out_specs=(vmem, vmem, vmem),
        scratch_shapes=[pltpu.VMEM(shape, dtype) for shape, dtype in scratch]
        + [pltpu.SemaphoreType.DMA((128,)), pltpu.SemaphoreType.DMA((128,))],
        compiler_params=pltpu.CompilerParams(
            collective_id=0, has_side_effects=True, vmem_limit_bytes=60 * 1024 * 1024
        ),
    )(chosen, route.reshape(64, 2 * sr), basis, strain)


def solution(mesh, dims=(8, 256, 256, BLOCK)):
    return jax.shard_map(
        functools.partial(local, dims),
        mesh=mesh,
        in_specs=(P("samp", "term"), P(("samp", "term"), None), P(), P()),
        out_specs=(P("samp", "term"), P(None, "term"), P(None, "term")),
        check_vma=False,
    )
```

```python
import functools

import jax
import jax.numpy as jnp
from jax import lax
from jax.experimental import pallas as pl
from jax.experimental.pallas import tpu as pltpu
from jax.sharding import PartitionSpec as P

BLOCK = 64
STEPS = 3
EPS = 1e-06
MESH = pl.DeviceIdType.MESH
HIGHEST = lax.Precision.HIGHEST
F32 = jnp.float32
BF16 = jnp.bfloat16


def nn(a, b, precision=None):
    return lax.dot_general(
        a, b, (((1,), (0,)), ((), ())), precision=precision, preferred_element_type=F32
    )


def nt(a, b, precision=None):
    return lax.dot_general(
        a, b, (((1,), (1,)), ((), ())), precision=precision, preferred_element_type=F32
    )


def tn(a, b):
    return lax.dot_general(a, b, (((0,), (0,)), ((), ())), preferred_element_type=F32)


def iota(shape, dim):
    return lax.broadcasted_iota(jnp.int32, shape, dim)


def ones_where(mask):
    return jnp.where(mask, 1.0, 0.0).astype(BF16)


def split(v):
    hi = v.astype(BF16)
    return hi, (v - hi.astype(F32)).astype(BF16)


class Bulk:
    def __init__(self, view, send_sem, recv_sem):
        self.view, self.send_sem, self.recv_sem = view, send_sem, recv_sem

    def wait_send(self):
        pltpu.make_async_copy(self.view, self.view, self.send_sem).wait()

    def wait_recv(self):
        pltpu.make_async_copy(self.view, self.view, self.recv_sem).wait()


def inverse_factor(a, width=8):
    n = a.shape[0]
    width = min(width, n)
    rows, cols = iota((n, n), 0), iota((n, n), 1)
    inv = jnp.where(rows == cols, 1.0, 0.0).astype(F32)
    for g in range(0, n, width):
        picked = range(g, g + width)
        columns = [jnp.broadcast_to(a[:, j : j + 1], (n, n)) for j in picked]
        rows_a = [a[j : j + 1, :] for j in picked]
        rows_i = [inv[j : j + 1, :] for j in picked]
        drop_a = drop_i = 0.0
        for i, j in enumerate(picked):
            scale = 1.0 / columns[i][j : j + 1, :]
            unit_a, unit_i = rows_a[i] * scale, rows_i[i] * scale
            below = jnp.where(rows > j, columns[i], 0.0)
            for m in range(i + 1, width):
                factor = columns[i][g + m : g + m + 1, :]
                rows_a[m] = rows_a[m] - factor * unit_a
                rows_i[m] = rows_i[m] - factor * unit_i
                columns[m] = columns[m] - below * (columns[m][j : j + 1, :] * scale)
            drop_a, drop_i = drop_a + below * unit_a, drop_i + below * unit_i
        a, inv = a - drop_a, inv - drop_i
    diag = jnp.sum(jnp.where(rows == cols, a, 0.0), axis=1, keepdims=True)
    return inv / jnp.sqrt(diag)


def body(
    dims, chosen, route, basis, strain, residual, coefs, scores,
    ptp, prs, psum, pry, ptf, out_h, mid_h, in_h, out_l, mid_l, in_l, pit, btg, rg, lo, rlo, pa,
    g_in, g_r, g_z, g_out, x_in, x_r, x_z, x_out, v_in, v_r, v_z, v_out, h_in, h_r, h_s, h_z,
    c_own, c_send, c_r, c_s, c_z, cg, sx, sg, wi, wm, wtm, index, ss, rs,
):
    rk, slab, tslab, bl = dims
    nr, q4, sr = 128 * rk, 32 * rk, 8 * rk
    p3, p2 = 3 * bl, 2 * bl
    half, group, wide = 2 * tslab, tslab // 2, slab // 2
    total = 8 * nr
    s, t = lax.axis_index("samp"), lax.axis_index("term")
    z, c = s // 2, lax.rem(s, 2)
    y, x = t // 4, lax.rem(t, 4)

    def at_x(d):
        return (s, y * 4 + lax.rem(x + d, 4))

    def at_y(d):
        return (s, lax.rem(y + d, 4) * 4 + x)

    def at_s(d):
        return (lax.rem(s + d, 8), t)

    def at_z(d):
        return (lax.rem(z + d, 4) * 2 + c, t)

    partner = (z * 2 + 1 - c, t)

    used = [0]

    def sems(n):
        used[0] += n
        return used[0] - n

    def copy(src, dst, k, dev):
        return pltpu.make_async_remote_copy(
            src_ref=src, dst_ref=dst, send_sem=ss.at[k], recv_sem=rs.at[k],
            device_id=dev, device_id_type=MESH,
        )

    def start(copies):
        for one in copies:
            one.start()
        return copies

    pending, awaited = [], []

    def wait_recv(copies):
        for one in copies:
            one.wait_recv()
            awaited[:] = [other for other in awaited if other is not one]

    def track(copies):
        pending.extend(copies)
        awaited.extend(copies)
        return copies

    def go(copies):
        return start(track(copies))

    def finish():
        wait_recv(list(awaited))
        for one in pending:
            one.wait_send()

    barrier = pltpu.get_barrier_semaphore()

    def greet(dev):
        pl.semaphore_signal(barrier, inc=1, device_id=dev, device_id_type=MESH)

    for d in (1, 2, 3):
        greet(at_x(d))
        greet(at_y(d))
    for d in range(1, 8):
        greet(at_s(d))

    rows = iota((p3, tslab), 0)
    which = jnp.where(rows < bl, chosen[0], jnp.where(rows < p2, chosen[1], chosen[2]))
    target = which * bl + lax.rem(rows, bl) - t * tslab
    select = ones_where(iota((p3, tslab), 1) == target)
    for q in range(4):
        ptp[q] = nt(select, basis[q * q4 : (q + 1) * q4, :]).astype(BF16)

    bits, fold = nr.bit_length() - 1, 5
    ahead = ones_where(
        (iota((2 * sr, 2 * sr), 0) < iota((2 * sr, 2 * sr), 1))
        & ((iota((2 * sr, 2 * sr), 0) >= sr) == (iota((2 * sr, 2 * sr), 1) >= sr))
    )
    own = route[pl.ds(s * 8 + t // 2, 1), :]
    own = jnp.where(lax.rem(t, 2) == 1, own[:, sr:], own[:, :sr]) >> bits
    to = iota((8, sr), 0) == own
    place = nn(ones_where(to), ahead[:sr, :sr]) + (iota((8, sr), 0) * rk).astype(F32)
    place = jnp.sum(jnp.where(to, place, 0.0), axis=0, keepdims=True)
    order = ones_where(iota((sr, sr), 0).astype(F32) == place)

    def packed(v):
        pair = [v[:, n * wide : (n + 1) * wide].reshape(8, rk, wide) for n in (0, 1)]
        return jnp.stack(pair, axis=1).reshape(8, 2 * rk, wide).astype(BF16)

    def unpacked(v):
        v = v.astype(F32).reshape(32, 2, rk, wide)
        return jnp.concatenate([v[:, n].reshape(q4, wide) for n in (0, 1)], axis=1).astype(BF16)

    def sort_slab(j, carry):
        for k in range(4):
            at = pl.multiple_of((j * 4 + k) * slab, slab)
            hi, low = split(strain[:, pl.ds(at, slab)])
            out_h[j, :, k] = packed(nn(order, hi))
            out_l[j, :, k] = packed(nn(order, low))
        return carry

    lax.fori_loop(0, 4, sort_slab, 0)

    hit = (route[...] >> bits) == s
    code = jnp.where(hit, nn(ones_where(hit), ahead) + 1.0, 0.0).astype(BF16)
    spot = route[...] & (nr - 1)
    high, low = (spot >> fold).astype(F32).astype(BF16), (spot & ((1 << fold) - 1)).astype(F32).astype(BF16)
    at = iota((q4, 64), 0)
    px, ps = at // sr, lax.rem(at // rk, 8)
    back = iota((q4, 2 * sr), 0)
    half_of = lax.rem(back // sr, 2) == (iota((q4, 2 * sr), 1) >= sr).astype(jnp.int32)
    turn = (lax.rem(back, rk) + 1).astype(F32)
    every = jnp.ones((8, 2 * sr), BF16)
    for q in range(4):
        pick = ones_where(iota((q4, 64), 1) == ps * 8 + q * 2 + px // 2)
        here = half_of & (nn(pick, code) == turn)
        big = nt(every, jnp.where(here, nn(pick, high), 0.0).astype(BF16))
        small = nt(every, jnp.where(here, nn(pick, low), 0.0).astype(BF16))
        index[:, q * q4 : (q + 1) * q4] = (big[:1] * (1 << fold) + small[:1]).astype(jnp.int32)

    pl.semaphore_wait(barrier, 13)

    k = sems(3)
    p_1 = go([copy(ptp.at[lax.rem(y + d, 4)], prs.at[d - 1], k + d - 1, at_y(d)) for d in (1, 2, 3)])

    to_s, to_x = {}, {}

    def send_z(low, j):
        src, dst = ((out_h, mid_h), (out_l, mid_l))[low]
        k = sems(1)

        def scatter(d, carry):
            dev = at_s(d)
            copy(src.at[j, dev[0]], dst.at[j, s], k, dev).start()
            return carry

        lax.fori_loop(1, 8, scatter, 0)
        to_s[low, j] = track([Bulk(dst.at[j, pl.ds(0, 7)], ss.at[k], rs.at[k])])
        dst[j, s] = src[j, s]

    def send_x(low, j):
        src, dst = ((mid_h, in_h), (mid_l, in_l))[low]
        wait_recv(to_s[low, j])
        k = sems(3)
        to_x[low, j] = go([copy(src.at[j, :, lax.rem(x + d, 4)], dst.at[j, x], k + d - 1, at_x(d)) for d in (1, 2, 3)])
        dst[j, x] = src[j, :, x]

    send_z(0, 0)
    send_z(0, 1)

    def build(q, carry):
        at = pl.multiple_of(q * q4, q4)
        pit[pl.ds(at, q4), :] = ones_where(iota((q4, nr), 0) + at == index[...])
        return carry

    lax.fori_loop(0, 4, build, 0)
    eye = ones_where(iota((tslab, tslab), 0) == iota((tslab, tslab), 1))
    bt = nt(eye, basis[...]).astype(BF16)
    btg[pl.ds(pl.multiple_of(x * tslab, tslab), tslab), :] = nn(bt, pit[...]).astype(BF16)

    own_rows = pl.ds(pl.multiple_of(y * q4, q4), q4)
    piece = tslab // 4
    b_out, b_on, r_out, r_on = [], [], [], []

    def b_view(slot, i):
        return btg.at[pl.ds(pl.multiple_of(slot * tslab + i * piece, piece), piece), :]

    def r_view(slot, j):
        return rg.at[j, pl.ds(pl.multiple_of(slot * q4, q4), q4), :]

    def ring_out(view, i, at, dev):
        k = sems(2)
        return go([copy(view(at, i), view(at, i), k + n, dev(1 + 2 * n)) for n in (0, 1)])

    def ring_on(view, i, at, dev, out):
        wait_recv([out[i // 2]])
        slot = lax.rem(at + (3, 1)[i // 2], 4)
        k = sems(1)
        return go([copy(view(slot, i), view(slot, i), k, dev((1, 3)[i // 2]))])

    def send_b(i):
        b_out.append(ring_out(b_view, i, x, at_x))

    def pass_b(i):
        b_on.append(ring_on(b_view, i, x, at_x, b_out[i]))

    def send_r(j):
        wait_recv(to_x[0, j])
        rg[j, own_rows, :] = unpacked(in_h[j])
        r_out.append(ring_out(r_view, j, y, at_y))

    def pass_r(j):
        r_on.append(ring_on(r_view, j, y, at_y, r_out[j]))

    send_b(0)
    send_x(0, 0)
    send_z(0, 2)
    wait_recv(p_1)
    psum[...] = ptp[y] + prs[0] + (prs[1] + prs[2])
    k = sems(3)
    p_2 = go([copy(psum, pry.at[d - 1], k + d - 1, at_x(d)) for d in (1, 2, 3)])
    send_b(1)
    send_x(0, 1)
    send_z(0, 3)
    send_r(0)
    pass_b(0)
    wait_recv(p_2)
    ptf[y] = psum[...] + pry[0] + (pry[1] + pry[2])
    k = sems(3)
    p_3 = go([copy(ptf.at[y], ptf.at[y], k + d - 1, at_y(d)) for d in (1, 2, 3)])
    send_x(0, 2)
    send_z(1, 0)
    send_b(2)
    send_r(1)
    pass_r(0)
    pass_b(1)
    send_x(0, 3)
    send_z(1, 1)
    send_b(3)

    def reduce_pair(src, got, k):
        return go([copy(src.at[1 - c], got, k, partner)])

    def reduce_ring(src, got, parts, k, pair):
        wait_recv(pair)
        parts[z] = (src[c].astype(F32) + got[...].astype(F32)).astype(parts.dtype)
        return go([copy(parts.at[z], parts.at[z], k + d - 1, at_z(d)) for d in (1, 2, 3)])

    def reduce_back(parts, out, k, around):
        wait_recv(around)
        four = [parts[n].astype(F32) for n in range(4)]
        out[c] = ((four[0] + four[1]) + (four[2] + four[3])).astype(out.dtype)
        return go([copy(out.at[c], out.at[c], k, partner)])

    wait_recv(p_3)
    at = 0
    for i in range(3):
        for j in range(i + 1):
            acc = None
            for q in range(4):
                one = nt(ptf[q, i * bl : (i + 1) * bl, :], ptf[q, j * bl : (j + 1) * bl, :])
                acc = one if acc is None else acc + one
            g_in[at // 3, at % 3] = acc
            at += 1
    g_1 = reduce_pair(g_in, g_r, sems(1))
    send_r(2)
    pass_r(1)
    pass_b(2)
    g_2 = reduce_ring(g_in, g_r, g_z, sems(3), g_1)
    send_z(1, 2)
    send_z(1, 3)
    acc = None
    for q in range(4):
        one = nn(ptf[q], pit[q * q4 : (q + 1) * q4, :])
        acc = one if acc is None else acc + one
    pa[...] = acc.astype(BF16)
    send_r(3)
    pass_r(2)
    pass_b(3)
    g_3 = reduce_back(g_z, g_out, sems(1), g_2)
    for j in range(4):
        send_x(1, j)
    pass_r(3)

    def lows_on():
        for j in range(4):
            wait_recv(to_x[1, j])
            lo[j] = unpacked(in_l[j])
        k = sems(3)
        rlo[own_rows, :] = lo[y]
        return go([copy(lo.at[lax.rem(y + d, 4)], rlo.at[own_rows, :], k + d - 1, at_y(d)) for d in (1, 2, 3)])

    def left_over(copies):
        return [got for got in copies if any(got is other for other in awaited)]

    def part(ref, zz, *lead):
        return ref.at[(*lead, pl.ds(pl.multiple_of(zz * group, group), group), slice(None))]

    def cross_pair(v, src, got):
        rows = v.shape[0] // 2
        src[0] = v[:rows].astype(src.dtype)
        src[1] = v[rows:].astype(src.dtype)
        return reduce_pair(src, got, sems(1))

    for i in range(4):
        wait_recv(left_over(b_out[i] + b_on[i]))
    other_half = pl.ds(pl.multiple_of((1 - c) * half, half), half)
    own_half = pl.ds(pl.multiple_of(c * half, half), half)
    ck, cz = sems(4), sems(12)
    c_1, c_2 = [], []

    def correlate(j):
        wait_recv(left_over(r_out[j] + r_on[j]))
        c_send[j] = nn(btg[other_half, :], rg[j]).astype(BF16)
        c_1.append(go([copy(c_send.at[j], c_r.at[j], ck + j, partner)]))
        c_own[j] = nn(btg[own_half, :], rg[j])

    def pass_on(j):
        wait_recv(c_1[j])
        both = c_own[j] + c_r[j].astype(F32)
        c_own[j] = both
        c_s[j] = both.astype(BF16)
        c_2.append(
            go([copy(part(c_s, lax.rem(z + d, 4), j), c_z.at[j, d - 1], cz + 3 * j + d - 1, at_z(d)) for d in (1, 2, 3)])
        )

    hk = sems(1)
    h_in[1] = nt(btg[other_half, :], pa[:p2, :]).astype(BF16)
    h_1 = go([copy(h_in.at[1], h_r, hk, partner)])
    h_in[0] = nt(btg[own_half, :], pa[:p2, :]).astype(BF16)
    correlate(0)
    wait_recv(h_1)
    h_s[...] = (h_in[0].astype(F32) + h_r[...].astype(F32)).astype(BF16)
    k = sems(3)
    h_2 = go([copy(part(h_s, lax.rem(z + d, 4)), h_z.at[d - 1], k + d - 1, at_z(d)) for d in (1, 2, 3)])
    correlate(1)
    pass_on(0)
    for j in range(4):
        wait_recv(left_over(r_out[j] + r_on[j]))
    x_1 = cross_pair(nn(pa[:p2, :], rg[y]), x_in, x_r)
    x_2 = reduce_ring(x_in, x_r, x_z, sems(3), x_1)
    lows = lows_on()

    wait_recv(g_3)

    def factor(i, a):
        wi[i] = inverse_factor(a)

    def rest(i, j):
        return g_out[(i * (i + 1) // 2 + j) // 3, (i * (i + 1) // 2 + j) % 3] / total

    factor(0, rest(0, 0))
    w00 = wi[0]
    l10, l20 = nt(rest(1, 0), w00, HIGHEST), nt(rest(2, 0), w00, HIGHEST)
    pass_on(1)
    correlate(2)
    x_3 = reduce_back(x_z, x_out, sems(1), x_2)
    factor(1, rest(1, 1) - nt(l10, l10, HIGHEST))
    pass_on(2)
    correlate(3)
    w11 = wi[1]
    l21 = nt(rest(2, 1) - nt(l20, l10, HIGHEST), w11, HIGHEST)
    factor(2, rest(2, 2) - nt(l20, l20, HIGHEST) - nt(l21, l21, HIGHEST))
    pass_on(3)
    wait_recv(lows)
    v_1 = cross_pair(nn(pa[...], rg[y]) + nn(pa[...], rlo[...]), v_in, v_r)
    w22 = wi[2]
    w10 = -nn(w11, nn(l10, w00, HIGHEST), HIGHEST)
    w20 = -nn(w22, nn(l20, w00, HIGHEST) + nn(l21, w10, HIGHEST), HIGHEST)
    w21 = -nn(w22, nn(l21, w11, HIGHEST), HIGHEST)
    zero = jnp.zeros((bl, bl), F32)
    wm[...] = jnp.concatenate(
        [
            jnp.concatenate([w00, zero, zero], axis=1),
            jnp.concatenate([w10, w11, zero], axis=1),
            jnp.concatenate([w20, w21, w22], axis=1),
        ],
        axis=0,
    )
    eye3 = jnp.where(iota((p3, p3), 0) == iota((p3, p3), 1), 1.0, 0.0).astype(F32)
    wtm[...] = nt(eye3, wm[...], HIGHEST)
    wait_recv(x_3)
    cross = jnp.concatenate([x_out[0], x_out[1]], axis=0).astype(F32) / total
    coef = nn(wm[:p2, :p2], cross, HIGHEST)
    cg[y] = coef.astype(BF16)
    k = sems(3)
    cg_1 = go([copy(cg.at[y], cg.at[y], k + d - 1, at_y(d)) for d in (1, 2, 3)])
    v_2 = reduce_ring(v_in, v_r, v_z, sems(3), v_1)
    for q in range(4):
        at = slice(q * q4, (q + 1) * q4)
        residual[at, :] = nn(pit[at, :], rg[y]) + nn(pit[at, :], rlo[...])

    def settle():
        wait_recv(v_3)
        full = jnp.concatenate([v_out[0], v_out[1]], axis=0) / total
        coef = nn(wm[...], full, HIGHEST)
        coefs[...] = coef
        y_hi, y_lo = split(nn(wtm[...], coef, HIGHEST))
        for q in range(4):
            at = slice(q * q4, (q + 1) * q4)
            residual[at, :] = residual[at, :] - (tn(ptf[q], y_hi) + tn(ptf[q], y_lo))

    wait_recv(h_2)
    four = [v.astype(F32) for v in (part(h_s, z)[...], h_z[0], h_z[1], h_z[2])]
    h_all = (four[0] + four[1]) + (four[2] + four[3])
    hn = nt(h_all, wm[:p2, :p2], HIGHEST).astype(BF16)
    first = jnp.where(iota((group, p2), 1) < bl, hn.astype(F32), 0.0).astype(BF16)
    wait_recv(cg_1)
    sums = [None] * 3
    for j in range(4):
        wait_recv(c_2[j])
        c0 = part(c_own, z, j)[...] + c_z[j, 0].astype(F32) + (c_z[j, 1].astype(F32) + c_z[j, 2].astype(F32))
        for i, v in enumerate((c0, c0 - nn(first, cg[j]), c0 - nn(hn, cg[j]))):
            sums[i] = v * v if sums[i] is None else sums[i] + v * v
    own_group = c * 4 + z
    per = group // bl
    rows8, lanes8 = iota((8, 128), 0), iota((8, 128), 1)
    tile = jnp.zeros((8, 128), F32)
    for i in range(3):
        for b in range(per):
            value = jnp.sum(sums[i][b * bl : (b + 1) * bl, :], axis=(0, 1), keepdims=True)
            spot = (rows8 == i) & (lanes8 == lax.rem(own_group, 2) * per + b)
            tile = jnp.where(spot, value, tile)
    sx[x] = tile
    v_3 = reduce_back(v_z, v_out, sems(1), v_2)
    k = sems(3)
    s_1 = go([copy(sx.at[x], sx.at[x], k + d - 1, at_x(d)) for d in (1, 2, 3)])
    wait_recv(s_1)
    sg[s] = (sx[0] + sx[1]) + (sx[2] + sx[3])
    ks = sems(1)

    def tell(d, carry):
        copy(sg.at[s], sg.at[s], ks, at_s(d)).start()
        return carry

    lax.fori_loop(1, 8, tell, 0)
    settle()
    wait_recv(track([Bulk(sg.at[pl.ds(0, 7)], ss.at[ks], rs.at[ks])]))
    out = jnp.zeros((8, 128), F32)
    for i in range(2):
        grp = 2 * x + i
        out = out + sg[lax.rem(grp, 4) * 2 + grp // 4]
    out = jnp.sqrt(out / (bl * 16 * slab) + EPS)
    scores[...] = out[:3, : 2 * per]

    finish()


def local(dims, basis, strain, route, chosen):
    rk, slab, tslab, bl = dims
    nr, q4, sr = 128 * rk, 32 * rk, 8 * rk
    p3, p2 = 3 * bl, 2 * bl
    half, group = 2 * tslab, tslab // 2
    vmem = pl.BlockSpec(memory_space=pltpu.VMEM)
    scratch = [
        ((4, p3, q4), BF16), ((3, p3, q4), BF16), ((p3, q4), BF16), ((3, p3, q4), BF16), ((4, p3, q4), BF16),
        *[((4, 8, 4, 2 * rk, slab // 2), BF16), ((4, 8, 4, 2 * rk, slab // 2), BF16), ((4, 4, 8, 2 * rk, slab // 2), BF16)] * 2,
        ((nr, nr), BF16), ((4 * tslab, nr), BF16),
        ((4, nr, slab), BF16), ((4, q4, slab), BF16), ((nr, slab), BF16), ((p3, nr), BF16),
        ((2, 3, bl, bl), F32), ((3, bl, bl), F32), ((4, 3, bl, bl), F32), ((2, 3, bl, bl), F32),
        ((2, bl, slab), BF16), ((bl, slab), BF16), ((4, bl, slab), BF16), ((2, bl, slab), BF16),
        ((2, p3 // 2, slab), F32), ((p3 // 2, slab), F32), ((4, p3 // 2, slab), F32), ((2, p3 // 2, slab), F32),
        ((2, half, p2), BF16), ((half, p2), BF16), ((half, p2), BF16), ((3, group, p2), BF16),
        ((4, half, slab), F32), ((4, half, slab), BF16), ((4, half, slab), BF16), ((4, half, slab), BF16),
        ((4, 3, group, slab), BF16), ((4, p2, slab), BF16), ((4, 8, 128), F32), ((8, 8, 128), F32),
        ((3, bl, bl), F32), ((p3, p3), F32), ((p3, p3), F32), ((1, nr), jnp.int32),
    ]
    return pl.pallas_call(
        functools.partial(body, dims),
        out_shape=(
            jax.ShapeDtypeStruct((nr, slab), F32),
            jax.ShapeDtypeStruct((p3, slab), F32),
            jax.ShapeDtypeStruct((3, tslab // bl), F32),
        ),
        in_specs=[pl.BlockSpec(memory_space=pltpu.SMEM), vmem, vmem, vmem],
        out_specs=(vmem, vmem, vmem),
        scratch_shapes=[pltpu.VMEM(shape, dtype) for shape, dtype in scratch]
        + [pltpu.SemaphoreType.DMA((128,)), pltpu.SemaphoreType.DMA((128,))],
        compiler_params=pltpu.CompilerParams(
            collective_id=0, has_side_effects=True, vmem_limit_bytes=60 * 1024 * 1024
        ),
    )(chosen, route.reshape(64, 2 * sr), basis, strain)


def solution(mesh, dims=(8, 256, 256, BLOCK)):
    return jax.shard_map(
        functools.partial(local, dims),
        mesh=mesh,
        in_specs=(P("samp", "term"), P(("samp", "term"), None), P(), P()),
        out_specs=(P("samp", "term"), P(None, "term"), P(None, "term")),
        check_vma=False,
    )
```
